128 devices in a mesh: sec: 2 (over core), dev: 64 (over z, x, y).
Axes of the slice: x: 4, y: 4, z: 4, core: 2. Of those that a mesh axis runs over, the one named last changes fastest.
Arguments:
- hidden_in: bfloat16 [2, 16, 4096], P('sec'), may hold values from -0.3125 to 0.3125
- queries: bfloat16 [2, 64, 16, 128], P('sec', 'dev'), may hold values from -4 to 4
- key_cache: bfloat16 [2, 64, 4096, 128], P('sec', 'dev'), may hold values from -12 to 12
- value_cache: bfloat16 [2, 64, 4096, 128], P('sec', 'dev'), may hold values from -6 to 6
- kv_lengths: int32 [2, 16], P('sec'), may hold values from 2 to 4096, as said below
- route_ids: int32 [2, 16, 8], replicated, may hold values from 0 to 63, all different within a row; in each aligned block of 16 rows (0 to 15, 16 to 31, ..., all dimensions but the last counted through in order) at most 4 rows name the same one
- out_weight: bfloat16 [8192, 4096], P('dev'), may hold values from -0.0625 to 0.0625
- norm_gain: bfloat16 [4096], replicated, may hold values from 0.099609375 to 1.8984375
- router_weight: bfloat16 [4096, 64], replicated, may hold values from -0.1875 to 0.1875
- w_gate: bfloat16 [64, 4096, 1536], P('dev', None, 'sec'), may hold values from -0.09375 to 0.09375
- w_up: bfloat16 [64, 4096, 1536], P('dev', None, 'sec'), may hold values from -0.09375 to 0.09375
- w_down: bfloat16 [64, 1536, 4096], P('dev', 'sec'), may hold values from -0.15625 to 0.15625
Outputs:
- mixed: bfloat16 [2, 16, 4096], P('sec', None, 'dev')
The draws below stay inside these ranges and needn't reach their ends.
Inputs may be any that keep to these rules, and one draw needn't show every extreme that they name: `route_ids`: no expert is chosen by more than 4 tokens of one micro-batch, and in some micro-batch some expert is chosen by exactly 4. `kv_lengths`: some sequence uses all 4096 positions.
All inputs are finite; a program needn't handle non-finite values.
Results may differ from the reference program's by a relative error of at most 0.018.
Values may be sent and summed in bfloat16 or wider, within the bound.
A program may use at most 128 MiB of HBM per device.

```python
import math
import jax
import jax.numpy as jnp
import numpy as np
from jax import lax

D = 4096
HEADS = 64
KV_HEADS = 4
HEAD_DIM = 128
FF = 1536
TOPK = 8
SEQS = 16
KV_LEN = 4096
EXPERTS = 64
PIECES = 64
ROWS = 32
CAP = 4


def draw_queries(key, part):
    key = jax.random.fold_in(key, 11)
    values = jnp.clip(jax.random.normal(key, (2, PIECES, HEADS // KV_HEADS, HEAD_DIM)), -4.0, 4.0)
    return values.astype(jnp.bfloat16)


def draw_key_cache(key, part):
    key = jax.random.fold_in(key, 12)
    values = jnp.clip(jax.random.normal(key, (2, PIECES, KV_LEN, HEAD_DIM)), -4.0, 4.0)
    return values.astype(jnp.bfloat16)


def draw_kv_lengths(key, part):
    key = jax.random.fold_in(key, 13)
    first_key, second_key = jax.random.split(key)
    lengths = jax.random.randint(first_key, (2 * SEQS,), 2, KV_LEN + 1, dtype=jnp.int32)
    chosen = jax.random.randint(second_key, (), 0, 2 * SEQS, dtype=jnp.int32)
    filled = jnp.where(jnp.arange(2 * SEQS, dtype=jnp.int32) == chosen, KV_LEN, lengths)
    return filled.reshape(2, SEQS).astype(jnp.int32)


def block_levels(rng, extent, pieces, low, top_value):
    loudness = 1.0
    for dim, blocks in pieces:
        draws = jax.random.uniform(jax.random.fold_in(jax.random.fold_in(rng, 6), dim), (blocks,), jnp.float32, low / len(pieces), top_value / len(pieces))
        loudness = loudness * jnp.repeat(jnp.exp(draws), extent[dim] // blocks).reshape((-1,) + (1,) * (len(extent) - 1 - dim))
    return loudness


def routed_block(own_key, own, number, rows, number_of, top, limit, slope):
    ranking = jax.random.permutation(own_key, number_of)
    crowded, ordinary = load_shares(number_of, rows * top, limit, slope, True), load_shares(number_of, rows * top, limit, slope, False)
    places = jnp.arange(number_of)

    def named(tallies, rotation):
        used = int((tallies > 0).sum())
        fixed = max(1, used // 4)
        moved = fixed + (places - fixed + rotation * (used - fixed)) % max(1, number_of - fixed)
        return jnp.zeros((number_of,), jnp.int32).at[ranking[jnp.where(places < fixed, places, moved)]].set(jnp.asarray(tallies, jnp.int32))

    tallies = jnp.where(number % 4 == 0, named(crowded, number // 4), named(ordinary, number - number // 4 - 1))
    mixed = jax.random.permutation(jax.random.fold_in(own, 3), number_of)
    giver, sink = mixed[0:number_of // 2 * 2:2], mixed[1:number_of // 2 * 2:2]
    room = jnp.minimum(tallies[giver] - 1, limit - tallies[sink]) // 2
    room = jnp.where((giver == ranking[0]) | (sink == ranking[0]) | (tallies[sink] == 0), 0, jnp.maximum(room, 0))
    moved = jax.random.randint(jax.random.fold_in(own, 4), (number_of // 2,), 0, 1 << 20) % (room + 1)
    tallies = tallies.at[giver].add(-moved).at[sink].add(moved)
    items = jnp.searchsorted(jnp.cumsum(tallies), jnp.arange(rows * top), side="right").astype(jnp.int32)
    listing = items.reshape(top, rows).T
    listing = listing[jax.random.permutation(jax.random.fold_in(own, 1), rows)]
    rotation = jax.random.randint(jax.random.fold_in(own, 2), (rows, 1), 0, top)
    return jnp.take_along_axis(listing, (jnp.arange(top)[None, :] + rotation) % top, axis=1)


def load_shares(amount, total, bound, lean, full):
    weights = [(1 << 20) // math.isqrt(standing ** lean) + 1 for standing in range(1, amount + 1)]
    largest = bound if full else min(bound, max(-(-total // amount), total * weights[0] // sum(weights)))
    least = 1 if total - largest >= amount - 1 else 0
    holding, spare = [largest] + [least] * (amount - 1), total - largest - least * (amount - 1)
    while spare > 0:
        candidates = [i for i in range(1, amount) if holding[i] < largest] or [i for i in range(1, amount) if holding[i] < bound]
        whole, left = sum([weights[i] for i in candidates]), spare
        for i in candidates:
            addition = min(bound - holding[i], max(1, left * weights[i] // whole), spare)
            holding[i] = holding[i] + addition
            spare = spare - addition
    return np.array(holding)


def scatter_about(own_key, extent, scale, bound, shards=(), held_as=jnp.bfloat16):
    gain = block_levels(own_key, extent, shards, -0.22, 0.18) if shards else 1.0
    entries = jax.random.normal(own_key, extent, jnp.float32) * scale * gain
    return jnp.minimum(jnp.maximum(entries, -bound), bound).astype(held_as)


def setup_inputs(seed: int = 0) -> dict:
    seeds = jax.random.split(jax.random.key(seed), 13)
    hidden_in = scatter_about(seeds[0], (2, SEQS, D), 0.02, 0.3125, ((0, 2),))
    queries = draw_queries(jax.random.fold_in(seeds[12], 71), 0)
    key_cache = draw_key_cache(jax.random.fold_in(seeds[12], 71), 0)
    value_cache = scatter_about(seeds[3], (2, PIECES, KV_LEN, HEAD_DIM), 1.0, 6.0, ((0, 2), (1, 64)))
    kv_lengths = draw_kv_lengths(jax.random.fold_in(seeds[12], 71), 0)
    route_ids_keys = jax.random.split(jax.random.fold_in(seeds[5], 1), 2 * SEQS // SEQS)
    route_ids_turns = jax.random.permutation(jax.random.fold_in(seeds[5], 3), 2 * SEQS // SEQS)
    route_ids = jax.vmap(lambda own, number: routed_block(jax.random.fold_in(seeds[5], 2), own, number, SEQS, EXPERTS, TOPK, CAP, 2))(route_ids_keys, route_ids_turns).reshape((2, SEQS, TOPK))
    out_weight = scatter_about(seeds[6], (HEADS * HEAD_DIM, D), (HEADS * HEAD_DIM) ** -0.5, 0.0625, ((0, 64),))
    norm_gain = jnp.clip(1.0 + 0.18 * jax.random.normal(seeds[7], (D,), jnp.float32), 0.099609375, 1.8984375).astype(jnp.bfloat16)
    router_weight = scatter_about(seeds[8], (D, EXPERTS), (D // 4) ** -0.5, 0.1875)
    w_gate = scatter_about(seeds[9], (EXPERTS, D, FF), D ** -0.5, 0.09375, ((0, 64), (2, 2)))
    w_up = scatter_about(seeds[10], (EXPERTS, D, FF), D ** -0.5, 0.09375, ((0, 64), (2, 2)))
    w_down = scatter_about(seeds[11], (EXPERTS, FF, D), FF ** -0.5, 0.15625, ((0, 64), (1, 2)))
    return dict(hidden_in=hidden_in, queries=queries, key_cache=key_cache, value_cache=value_cache, kv_lengths=kv_lengths, route_ids=route_ids, out_weight=out_weight, norm_gain=norm_gain, router_weight=router_weight, w_gate=w_gate, w_up=w_up, w_down=w_down)


MASKED_SCORE = -1e+30
NORM_EPS = 1e-06

def reference(hidden_in, queries, key_cache, value_cache, kv_lengths, route_ids, out_weight, norm_gain, router_weight, w_gate, w_up, w_down):
    scores = jnp.einsum('spgh,splh->spgl', queries.astype(jnp.float32), key_cache.astype(jnp.float32), precision=lax.Precision.HIGHEST) * HEAD_DIM ** (-0.5)
    piece_lengths = jnp.repeat(kv_lengths, KV_HEADS, axis=1)
    is_valid = (jnp.arange(KV_LEN, dtype=jnp.int32)[None, None, :] < piece_lengths[:, :, None])[:, :, None, :]
    scores = jnp.where(is_valid, scores, MASKED_SCORE)
    row_max = lax.optimization_barrier(jnp.max(scores, axis=-1, keepdims=True))
    weights = jnp.where(is_valid, jnp.exp(scores - row_max), 0.0)
    probs = weights / lax.optimization_barrier(jnp.sum(weights, axis=-1, keepdims=True))
    head_out = jnp.einsum('spgl,splh->spgh', probs, value_cache.astype(jnp.float32), precision=lax.Precision.HIGHEST)
    attended = head_out.reshape(ROWS, HEADS * HEAD_DIM).astype(jnp.bfloat16)
    residual = hidden_in.reshape(ROWS, D).astype(jnp.float32) + jnp.dot(attended, out_weight, preferred_element_type=jnp.float32)
    normed = (residual * lax.rsqrt(lax.optimization_barrier(jnp.mean(residual * residual, axis=-1, keepdims=True)) + NORM_EPS) * norm_gain.astype(jnp.float32)).astype(jnp.bfloat16)
    logits = jnp.dot(normed, router_weight, preferred_element_type=jnp.float32)
    route_rows = route_ids.reshape(ROWS, TOPK)
    onehot = route_rows[:, :, None] == jnp.arange(EXPERTS, dtype=jnp.int32)[None, None, :]
    picked = lax.optimization_barrier(jnp.sum(jnp.where(onehot, logits[:, None, :], 0.0), axis=-1))
    sig_scores = jax.nn.sigmoid(picked)
    gates = sig_scores / lax.optimization_barrier(jnp.sum(sig_scores, axis=-1, keepdims=True))

    def expert_step(total, packed):
        gate_mat, up_mat, down_mat, expert_id = packed
        gate_proj = jnp.dot(normed, gate_mat, preferred_element_type=jnp.float32)
        up_proj = jnp.dot(normed, up_mat, preferred_element_type=jnp.float32)
        expert_hidden = (jax.nn.silu(gate_proj) * up_proj).astype(jnp.bfloat16)
        expert_out = jnp.dot(expert_hidden, down_mat, preferred_element_type=jnp.float32)
        row_share = lax.optimization_barrier(jnp.sum(jnp.where(route_rows == expert_id, gates, 0.0), axis=-1))
        return (total + expert_out * row_share[:, None], None)
    routed_sum, unused = lax.scan(expert_step, jnp.zeros((ROWS, D), jnp.float32), (w_gate, w_up, w_down, jnp.arange(EXPERTS, dtype=jnp.int32)))
    return (residual + routed_sum).astype(jnp.bfloat16).reshape(2, SEQS, D)
```

```python
import functools

import jax
import jax.numpy as jnp
from jax import lax
from jax.experimental import pallas as pl
from jax.experimental.pallas import tpu as pltpu
from jax.sharding import PartitionSpec as P

MASKED_SCORE = -1e30
NORM_EPS = 1e-06
MESH = pl.DeviceIdType.MESH
LANES = 128
CAP = 4
SIDE = 4
PLANE = SIDE * SIDE
RING_ORDER = (2, 1, 3, 0)


def hops(step):
    return min(step, SIDE - step)


def far_first(steps):
    return sorted(steps, key=lambda step: -sum(hops(part) for part in step))


PLANE_STEPS = far_first([(dx, dy) for dx in range(SIDE) for dy in range(SIDE)])
CUBE_STEPS = far_first(
    [(dz, dx, dy) for dz in range(SIDE) for dx in range(SIDE) for dy in range(SIDE)]
)


def layer_kernel(
    hidden_ref,
    query_ref,
    key_hbm,
    value_hbm,
    length_ref,
    route_ref,
    out_weight_hbm,
    gain_ref,
    router_hbm,
    gate_hbm,
    up_hbm,
    down_hbm,
    out_ref,
    key_buf,
    value_buf,
    out_weight_buf,
    router_buf,
    gate_buf,
    up_buf,
    down_buf,
    att_out,
    att_in,
    part_out,
    part_in,
    block_out,
    rows_in,
    own_half,
    other_half,
    half_in,
    comb_out,
    comb_in,
    load_sem,
    att_send,
    att_recv,
    part_send,
    part_recv,
    rows_send,
    rows_recv,
    half_send,
    half_recv,
    comb_send,
    comb_recv,
):
    s = lax.axis_index("sec")
    d = lax.axis_index("dev")
    z = d // PLANE
    x = lax.rem(d // SIDE, SIDE)
    y = lax.rem(d, SIDE)
    seqs = hidden_ref.shape[1]
    kv_span = key_buf.shape[0]
    head_dim = key_buf.shape[1]
    width = out_weight_buf.shape[1]
    rows = 2 * seqs
    chunk = width // SIDE
    chunk_blocks = chunk // LANES

    loads = [
        pltpu.make_async_copy(src, dst, load_sem.at[i])
        for i, (src, dst) in enumerate(
            (
                (key_hbm.at[0, 0], key_buf),
                (value_hbm.at[0, 0], value_buf),
                (out_weight_hbm, out_weight_buf),
                (gate_hbm.at[0], gate_buf),
                (up_hbm.at[0], up_buf),
                (router_hbm, router_buf),
                (down_hbm.at[0], down_buf),
            )
        )
    ]
    for load in loads:
        load.start()

    zs = [lax.rem(z + i, SIDE) for i in range(SIDE)]
    xs = [lax.rem(x + i, SIDE) for i in range(SIDE)]
    ys = [lax.rem(y + i, SIDE) for i in range(SIDE)]

    def at(dz, dx, dy):
        return zs[dz] * PLANE + xs[dx] * SIDE + ys[dy]

    barrier = pltpu.get_barrier_semaphore()
    for step in CUBE_STEPS[:-1]:
        pl.semaphore_signal(barrier, inc=1, device_id=(s, at(*step)), device_id_type=MESH)
    pl.semaphore_signal(barrier, inc=1, device_id=(1 - s, d), device_id_type=MESH)

    loads[0].wait()
    scores = lax.dot_general(
        query_ref[0, 0], key_buf[...], (((1,), (1,)), ((), ())), preferred_element_type=jnp.float32
    ) * head_dim ** (-0.5)
    length = length_ref[0, d // SIDE]
    is_valid = lax.broadcasted_iota(jnp.int32, scores.shape, 1) < length
    scores = jnp.where(is_valid, scores, MASKED_SCORE)
    top = jnp.max(scores, axis=-1, keepdims=True)
    weights = jnp.where(is_valid, jnp.exp(scores - top), 0.0).astype(jnp.bfloat16)
    total = jnp.sum(weights.astype(jnp.float32), axis=-1, keepdims=True)
    loads[1].wait()
    attended = jnp.dot(weights, value_buf[...], preferred_element_type=jnp.float32) / total
    att_out[...] = attended.reshape(att_out.shape)

    pl.semaphore_wait(barrier, SIDE * PLANE)
    seq = d // SIDE
    for dx, dy in PLANE_STEPS:
        in_plane = xs[dx] * SIDE + ys[dy]
        src = att_out.at[in_plane]
        dst = att_in.at[seq]

        def send_row(src=src, dst=dst, target=y * PLANE + in_plane):
            pltpu.make_async_remote_copy(
                src, dst, att_send, att_recv, device_id=(s, target), device_id_type=MESH
            ).start()

        if (dx, dy) == (0, 0):
            pl.when(y != z)(send_row)

            @pl.when(y == z)
            def _():
                pltpu.make_async_copy(src, dst, att_recv).start()
        else:
            send_row()

    routes = jnp.concatenate([route_ref[0], route_ref[1]], axis=0)
    chosen = jnp.sum((routes == d).astype(jnp.float32), axis=1, keepdims=True)
    row_a = lax.broadcasted_iota(jnp.int32, (rows, rows), 0)
    row_b = lax.broadcasted_iota(jnp.int32, (rows, rows), 1)
    chosen_row = jnp.sum(jnp.where(row_a == row_b, chosen, 0.0), axis=0, keepdims=True)
    before = (row_a < row_b) & (row_a // seqs == row_b // seqs)
    rank_row = jnp.sum(jnp.where(before, chosen, 0.0), axis=0, keepdims=True)
    slot = lax.broadcasted_iota(jnp.int32, (2 * CAP, rows), 0)
    token = lax.broadcasted_iota(jnp.int32, (2 * CAP, rows), 1)
    slot_batch = jnp.where(slot < CAP, s, 1 - s)
    picked = (
        (token // seqs == slot_batch)
        & (rank_row == lax.rem(slot, CAP).astype(jnp.float32))
        & (chosen_row > 0.5)
    )
    pick = jnp.where(picked, 1.0, 0.0).astype(jnp.bfloat16)

    experts = router_buf.shape[1]
    own_routes = route_ref[s]
    expert_lane = lax.broadcasted_iota(jnp.int32, (seqs, experts), 1)
    match = jnp.zeros((seqs, experts), jnp.float32)
    for k in range(own_routes.shape[1]):
        match = match + (own_routes[:, k : k + 1] == expert_lane).astype(jnp.float32)
    lower = lax.broadcasted_iota(jnp.int32, (seqs, seqs), 0) > lax.broadcasted_iota(
        jnp.int32, (seqs, seqs), 1
    )
    rank = jnp.dot(
        lower.astype(jnp.bfloat16), match.astype(jnp.bfloat16), preferred_element_type=jnp.float32
    )
    slots = experts * CAP
    spread = (
        lax.broadcasted_iota(jnp.int32, (experts, slots), 1) // CAP
        == lax.broadcasted_iota(jnp.int32, (experts, slots), 0)
    ).astype(jnp.float32)
    rank_slots = jnp.dot(
        rank.astype(jnp.bfloat16), spread.astype(jnp.bfloat16), preferred_element_type=jnp.float32
    )
    slot_lane = lax.rem(lax.broadcasted_iota(jnp.int32, (seqs, slots), 1), CAP)
    in_slot = rank_slots == slot_lane.astype(jnp.float32)

    loads[2].wait()
    pltpu.make_async_copy(att_in, att_in, att_recv).wait()
    head_rows = att_in[...].reshape(seqs, head_dim).astype(jnp.bfloat16)
    for dz in range(SIDE):
        base = pl.multiple_of(dz * chunk, chunk)
        partial = jnp.dot(
            head_rows, out_weight_buf[:, pl.ds(base, chunk)], preferred_element_type=jnp.float32
        ).astype(jnp.bfloat16)
        for j in range(chunk_blocks):
            part_out[dz * chunk_blocks + j] = partial[:, j * LANES : (j + 1) * LANES]
    for step in CUBE_STEPS:
        target = at(*step)
        src = part_out.at[target // 2]
        dst = part_in.at[d]
        if step == (0, 0, 0):
            pltpu.make_async_copy(src, dst, part_recv).start()
        else:
            pltpu.make_async_remote_copy(
                src, dst, part_send, part_recv, device_id=(s, target), device_id_type=MESH
            ).start()

    my_block = d // 2
    my_half = lax.rem(d, 2)
    lanes_at = pl.multiple_of(my_block * LANES, LANES)
    hidden_block = hidden_ref[0, :, pl.ds(lanes_at, LANES)].astype(jnp.float32)
    gain = gain_ref[...].astype(jnp.float32)
    gain_block = gain_ref[:, pl.ds(lanes_at, LANES)].astype(jnp.float32)

    pltpu.make_async_copy(part_in, part_in, part_recv).wait()
    residual = hidden_block
    for i in range(part_in.shape[0]):
        residual = residual + part_in[i].astype(jnp.float32)
    block_out[...] = (residual * gain_block).astype(jnp.bfloat16)

    for step in CUBE_STEPS:
        dst = rows_in.at[my_block, s]

        def send_block(dst=dst, target=at(*step), dz=step[0]):
            pltpu.make_async_remote_copy(
                block_out,
                dst,
                rows_send,
                rows_recv.at[dz],
                device_id=(my_half, target),
                device_id_type=MESH,
            ).start()

        if step == (0, 0, 0):
            pl.when(my_half != s)(send_block)

            @pl.when(my_half == s)
            def _():
                pltpu.make_async_copy(block_out, dst, rows_recv.at[0]).start()
        else:
            send_block()

    inverse_square = 1.0 / (gain * gain)
    gate_proj = jnp.zeros((rows, gate_buf.shape[1]), jnp.float32)
    up_proj = jnp.zeros((rows, gate_buf.shape[1]), jnp.float32)
    squares = jnp.zeros((rows, LANES), jnp.float32)
    loads[3].wait()
    loads[4].wait()
    for dz in (0, 1, 3, 2):
        plane = lax.rem(z + SIDE - dz, SIDE)
        arrived = rows_in.at[pl.ds(plane * chunk_blocks, chunk_blocks)]
        pltpu.make_async_copy(arrived, arrived, rows_recv.at[dz]).wait()
        tokens = jnp.concatenate(
            [rows_in[plane * chunk_blocks + j].reshape(rows, LANES) for j in range(chunk_blocks)],
            axis=1,
        )
        base = pl.multiple_of(plane * chunk, chunk)
        gate_proj = gate_proj + jnp.dot(
            tokens, gate_buf[pl.ds(base, chunk), :], preferred_element_type=jnp.float32
        )
        up_proj = up_proj + jnp.dot(
            tokens, up_buf[pl.ds(base, chunk), :], preferred_element_type=jnp.float32
        )
        wide = tokens.astype(jnp.float32)
        gain_part = gain_ref[:, pl.ds(base, chunk)].astype(jnp.float32)
        wide = wide * wide * (1.0 / (gain_part * gain_part))
        for j in range(chunk_blocks):
            squares = squares + wide[:, j * LANES : (j + 1) * LANES]
    scale = lax.rsqrt(jnp.sum(squares, axis=1, keepdims=True) / width + NORM_EPS)
    gate_proj = gate_proj * scale
    up_proj = up_proj * scale
    hidden = (gate_proj * jax.nn.sigmoid(gate_proj) * up_proj).astype(jnp.bfloat16)
    packed = jnp.dot(pick, hidden, preferred_element_type=jnp.float32).astype(jnp.bfloat16)

    loads[6].wait()

    def half_copy(order):
        plane = zs[RING_ORDER[order]]
        where = pl.ds(plane * chunk_blocks, chunk_blocks)
        return pltpu.make_async_remote_copy(
            other_half.at[where],
            half_in.at[where],
            half_send.at[order],
            half_recv.at[order],
            device_id=(1 - s, d),
            device_id_type=MESH,
        )

    def down(order):
        plane = zs[RING_ORDER[order]]
        base = pl.multiple_of(plane * chunk, chunk)
        product = jnp.dot(packed, down_buf[:, pl.ds(base, chunk)], preferred_element_type=jnp.float32)
        for j in range(chunk_blocks):
            block = product[:, j * LANES : (j + 1) * LANES]
            own_half[plane * chunk_blocks + j] = block[:CAP]
            other_half[plane * chunk_blocks + j] = block[CAP:]
        half_copy(order).start()

    def combine(order):
        dz = RING_ORDER[order]
        where = pl.ds(zs[dz] * chunk_blocks, chunk_blocks)
        half_copy(order).wait_recv()
        comb_out[where] = own_half[where] + half_in[where]
        for dx, dy in PLANE_STEPS:
            target = at(dz, dx, dy)
            src = comb_out.at[target // 2]
            dst = comb_in.at[d]
            if (dz, dx, dy) == (0, 0, 0):
                pltpu.make_async_copy(src, dst, comb_recv).start()
            else:
                pltpu.make_async_remote_copy(
                    src, dst, comb_send, comb_recv, device_id=(s, target), device_id_type=MESH
                ).start()

    down(0)
    for order in range(1, SIDE):
        down(order)
        combine(order - 1)
    combine(SIDE - 1)

    loads[5].wait()
    logits = jnp.zeros((seqs, experts), jnp.float32)
    own_tokens = jnp.concatenate([rows_in[k, s] for k in range(rows_in.shape[0])], axis=1)
    logits = jnp.dot(own_tokens, router_buf[...], preferred_element_type=jnp.float32)
    own_scale = jnp.where(s == 0, scale[:seqs], scale[seqs:])
    shares = match * jax.nn.sigmoid(logits * own_scale)
    gates = shares / jnp.sum(shares, axis=1, keepdims=True)
    gate_slots = jnp.where(
        in_slot,
        jnp.dot(
            gates, spread, precision=lax.Precision.HIGHEST, preferred_element_type=jnp.float32
        ),
        0.0,
    )

    pltpu.make_async_copy(comb_in, comb_in, comb_recv).wait()
    routed = jnp.dot(
        gate_slots,
        comb_in[...].reshape(slots, LANES),
        precision=lax.Precision.HIGHEST,
        preferred_element_type=jnp.float32,
    )
    mixed = residual + routed
    features = out_ref.shape[2]
    out_ref[0] = jnp.where(my_half == 0, mixed[:, :features], mixed[:, features:]).astype(
        out_ref.dtype
    )

    for order in range(SIDE):
        half_copy(order).wait_send()
    most = att_in.at[pl.ds(0, PLANE - 1)]
    pltpu.make_async_copy(most, most, att_send).wait()

    @pl.when(y != z)
    def _():
        pltpu.make_async_copy(att_in.at[0], att_in.at[0], att_send).wait()

    most = part_in.at[pl.ds(0, SIDE * PLANE - 1)]
    pltpu.make_async_copy(most, most, part_send).wait()
    pltpu.make_async_copy(most, most, rows_send).wait()

    @pl.when(my_half != s)
    def _():
        pltpu.make_async_copy(block_out, block_out, rows_send).wait()

    most = comb_in.at[pl.ds(0, SIDE * PLANE - 1)]
    pltpu.make_async_copy(most, most, comb_send).wait()


def body(
    hidden_in,
    queries,
    key_cache,
    value_cache,
    kv_lengths,
    route_ids,
    out_weight,
    norm_gain,
    router_weight,
    w_gate,
    w_up,
    w_down,
):
    seqs, width = hidden_in.shape[1:]
    kv_span, head_dim = key_cache.shape[2:]
    experts = router_weight.shape[1]
    hidden_units = w_gate.shape[2]
    devices = lax.axis_size("dev")
    blocks = width // LANES
    vmem = pl.BlockSpec(memory_space=pltpu.VMEM)
    hbm = pl.BlockSpec(memory_space=pl.ANY)
    smem = pl.BlockSpec(memory_space=pltpu.SMEM)
    dma = pltpu.SemaphoreType.DMA
    return pl.pallas_call(
        layer_kernel,
        out_shape=jax.ShapeDtypeStruct((1, seqs, width // devices), jnp.bfloat16),
        in_specs=[vmem, vmem, hbm, hbm, smem, vmem, hbm, vmem, hbm, hbm, hbm, hbm],
        out_specs=vmem,
        scratch_shapes=[
            pltpu.VMEM((kv_span, head_dim), jnp.bfloat16),
            pltpu.VMEM((kv_span, head_dim), jnp.bfloat16),
            pltpu.VMEM(out_weight.shape, jnp.bfloat16),
            pltpu.VMEM(router_weight.shape, jnp.bfloat16),
            pltpu.VMEM((width, hidden_units), jnp.bfloat16),
            pltpu.VMEM((width, hidden_units), jnp.bfloat16),
            pltpu.VMEM((hidden_units, width), jnp.bfloat16),
            pltpu.VMEM((seqs, 1, head_dim), jnp.float32),
            pltpu.VMEM((seqs, 1, head_dim), jnp.float32),
            pltpu.VMEM((blocks, seqs, LANES), jnp.bfloat16),
            pltpu.VMEM((devices, seqs, LANES), jnp.bfloat16),
            pltpu.VMEM((seqs, LANES), jnp.bfloat16),
            pltpu.VMEM((blocks, 2, seqs, LANES), jnp.bfloat16),
            pltpu.VMEM((blocks, CAP, LANES), jnp.float32),
            pltpu.VMEM((blocks, CAP, LANES), jnp.float32),
            pltpu.VMEM((blocks, CAP, LANES), jnp.float32),
            pltpu.VMEM((blocks, CAP, LANES), jnp.float32),
            pltpu.VMEM((devices, CAP, LANES), jnp.float32),
            dma((7,)),
            dma,
            dma,
            dma,
            dma,
            dma,
            dma((SIDE,)),
            dma((SIDE,)),
            dma((SIDE,)),
            dma,
            dma,
        ],
        compiler_params=pltpu.CompilerParams(
            collective_id=0, has_side_effects=True, vmem_limit_bytes=56 * 2**20
        ),
    )(
        hidden_in,
        queries,
        key_cache,
        value_cache,
        kv_lengths,
        route_ids,
        out_weight,
        norm_gain.reshape(1, width),
        router_weight,
        w_gate,
        w_up,
        w_down,
    )


def solution(mesh):
    placed = (
        P("sec", None, None),
        P("sec", "dev", None, None),
        P("sec", "dev", None, None),
        P("sec", "dev", None, None),
        P("sec", None),
        P(),
        P("dev", None),
        P(),
        P(),
        P("dev", None, "sec"),
        P("dev", None, "sec"),
        P("dev", "sec", None),
    )
    return jax.shard_map(
        body, mesh=mesh, in_specs=placed, out_specs=P("sec", None, "dev"), check_vma=False
    )
```

```python
import functools

import jax
import jax.numpy as jnp
from jax import lax
from jax.experimental import pallas as pl
from jax.experimental.pallas import tpu as pltpu
from jax.sharding import PartitionSpec as P

MASKED_SCORE = -1e30
NORM_EPS = 1e-06
MESH = pl.DeviceIdType.MESH
LANES = 128
CAP = 4
SIDE = 4
PLANE = SIDE * SIDE
RING_ORDER = (2, 1, 3, 0)


def hops(step):
    return min(step, SIDE - step)


def far_first(steps):
    return sorted(steps, key=lambda step: -sum(hops(part) for part in step))


PLANE_STEPS = far_first([(dx, dy) for dx in range(SIDE) for dy in range(SIDE)])
CUBE_STEPS = far_first(
    [(dz, dx, dy) for dz in range(SIDE) for dx in range(SIDE) for dy in range(SIDE)]
)


def layer_kernel(
    hidden_hbm,
    query_hbm,
    key_hbm,
    value_hbm,
    length_hbm,
    route_hbm,
    out_weight_hbm,
    gain_hbm,
    router_hbm,
    gate_hbm,
    up_hbm,
    down_hbm,
    out_ref,
    hidden_ref,
    query_ref,
    length_ref,
    route_ref,
    gain_ref,
    key_buf,
    value_buf,
    out_weight_buf,
    router_buf,
    gate_buf,
    up_buf,
    down_buf,
    att_out,
    att_in,
    part_out,
    part_in,
    block_out,
    rows_in,
    gain_buf,
    inverse_buf,
    comb_out,
    comb_in,
    load_sem,
    att_send,
    att_recv,
    part_send,
    part_recv,
    rows_send,
    rows_recv,
    comb_send,
    comb_recv,
):
    s = lax.axis_index("sec")
    d = lax.axis_index("dev")
    z = d // PLANE
    x = lax.rem(d // SIDE, SIDE)
    y = lax.rem(d, SIDE)
    seqs = hidden_ref.shape[0]
    kv_span = key_buf.shape[0]
    head_dim = key_buf.shape[1]
    width = out_weight_buf.shape[1]
    rows = 2 * seqs
    chunk = width // SIDE
    chunk_blocks = chunk // LANES

    loads = [
        pltpu.make_async_copy(src, dst, load_sem.at[i])
        for i, (src, dst) in enumerate(
            (
                (length_hbm, length_ref),
                (query_hbm.at[0, 0], query_ref),
                (key_hbm.at[0, 0], key_buf),
                (value_hbm.at[0, 0], value_buf),
                (route_hbm, route_ref),
                (out_weight_hbm, out_weight_buf),
                (gate_hbm.at[0], gate_buf),
                (up_hbm.at[0], up_buf),
                (router_hbm, router_buf),
                (down_hbm.at[0], down_buf),
                (hidden_hbm.at[0], hidden_ref),
                (gain_hbm, gain_ref),
            )
        )
    ]
    (
        length_load,
        query_load,
        key_load,
        value_load,
        route_load,
        out_weight_load,
        gate_load,
        up_load,
        router_load,
        down_load,
        hidden_load,
        gain_load,
    ) = loads
    zs = [lax.rem(z + i, SIDE) for i in range(SIDE)]
    xs = [lax.rem(x + i, SIDE) for i in range(SIDE)]
    ys = [lax.rem(y + i, SIDE) for i in range(SIDE)]

    def at(dz, dx, dy):
        return zs[dz] * PLANE + xs[dx] * SIDE + ys[dy]

    barrier = pltpu.get_barrier_semaphore()

    def greet(target):
        pl.semaphore_signal(barrier, inc=1, device_id=(s, target), device_id_type=MESH)

    for load in loads[:4]:
        load.start()
    pl.semaphore_signal(barrier, inc=1, device_id=(1 - s, d), device_id_type=MESH)
    for dz, dx in PLANE_STEPS[:-1]:
        greet(zs[dz] * PLANE + xs[dx] * SIDE + z)
    for dx, turn in PLANE_STEPS:
        if turn:
            greet(y * PLANE + xs[dx] * SIDE + zs[turn])
    pl.when(y != z)(lambda: greet(z * PLANE + x * SIDE + z))
    for load in loads[4:]:
        load.start()

    query_load.wait()
    length_load.wait()
    key_load.wait()
    scores = lax.dot_general(
        query_ref[...], key_buf[...], (((1,), (1,)), ((), ())), preferred_element_type=jnp.float32
    ) * head_dim ** (-0.5)
    length = length_ref[0, d // SIDE]
    is_valid = lax.broadcasted_iota(jnp.int32, scores.shape, 1) < length
    scores = jnp.where(is_valid, scores, MASKED_SCORE)
    top = jnp.max(scores, axis=-1, keepdims=True)
    weights = jnp.where(is_valid, jnp.exp(scores - top), 0.0).astype(jnp.bfloat16)
    total = jnp.sum(weights.astype(jnp.float32), axis=-1, keepdims=True)
    value_load.wait()
    attended = jnp.dot(weights, value_buf[...], preferred_element_type=jnp.float32) / total
    att_out[...] = attended.reshape(att_out.shape)

    pl.semaphore_wait(barrier, 2 * PLANE - SIDE + 1 - (y == z).astype(jnp.int32))
    seq = d // SIDE
    for dx, dy in PLANE_STEPS:
        in_plane = xs[dx] * SIDE + ys[dy]
        src = att_out.at[in_plane]
        dst = att_in.at[seq]

        def send_row(src=src, dst=dst, target=y * PLANE + in_plane):
            pltpu.make_async_remote_copy(
                src, dst, att_send, att_recv, device_id=(s, target), device_id_type=MESH
            ).start()

        if (dx, dy) == (0, 0):
            pl.when(y != z)(send_row)

            @pl.when(y == z)
            def _():
                pltpu.make_async_copy(src, dst, att_recv).start()
        else:
            send_row()

    route_load.wait()
    routes = jnp.concatenate([route_ref[0], route_ref[1]], axis=1)
    chosen_row = jnp.sum((routes == d).astype(jnp.float32), axis=0, keepdims=True)
    row_a = lax.broadcasted_iota(jnp.int32, (rows, rows), 0)
    row_b = lax.broadcasted_iota(jnp.int32, (rows, rows), 1)
    before = (row_a < row_b) & (row_a // seqs == row_b // seqs)
    rank_row = jnp.dot(
        jnp.broadcast_to(chosen_row, (2 * CAP, rows)).astype(jnp.bfloat16),
        before.astype(jnp.bfloat16),
        preferred_element_type=jnp.float32,
    )
    slot = lax.broadcasted_iota(jnp.int32, (2 * CAP, rows), 0)
    token = lax.broadcasted_iota(jnp.int32, (2 * CAP, rows), 1)
    slot_batch = jnp.where(lax.rem(slot // 2, 2) == 0, s, 1 - s)
    slot_rank = slot // CAP * 2 + lax.rem(slot, 2)
    picked = (
        (token // seqs == slot_batch)
        & (rank_row == slot_rank.astype(jnp.float32))
        & (chosen_row > 0.5)
    )
    pick = jnp.where(picked, 1.0, 0.0).astype(jnp.bfloat16)

    experts = router_buf.shape[0]
    own_routes = route_ref[s]
    expert_row = lax.broadcasted_iota(jnp.int32, (experts, seqs), 0)
    match_rows = jnp.zeros((experts, seqs), jnp.float32)
    for k in range(own_routes.shape[0]):
        match_rows = match_rows + (own_routes[k : k + 1] == expert_row).astype(jnp.float32)
    same = lax.broadcasted_iota(jnp.int32, (seqs, seqs), 0) == lax.broadcasted_iota(
        jnp.int32, (seqs, seqs), 1
    )
    match = lax.dot_general(
        same.astype(jnp.bfloat16),
        match_rows.astype(jnp.bfloat16),
        (((1,), (1,)), ((), ())),
        preferred_element_type=jnp.float32,
    )
    lower = lax.broadcasted_iota(jnp.int32, (seqs, seqs), 0) > lax.broadcasted_iota(
        jnp.int32, (seqs, seqs), 1
    )
    rank = jnp.dot(
        lower.astype(jnp.bfloat16), match.astype(jnp.bfloat16), preferred_element_type=jnp.float32
    )
    slots = experts * 2
    spread = (
        lax.broadcasted_iota(jnp.int32, (experts, slots), 1) // 2
        == lax.broadcasted_iota(jnp.int32, (experts, slots), 0)
    ).astype(jnp.float32)
    rank_slots = jnp.dot(
        rank.astype(jnp.bfloat16), spread.astype(jnp.bfloat16), preferred_element_type=jnp.float32
    )
    low_slot = lax.rem(lax.broadcasted_iota(jnp.int32, (seqs, slots), 1), 2).astype(jnp.float32)
    in_slot = jnp.concatenate([rank_slots == low_slot, rank_slots == low_slot + 2.0], axis=0)

    out_weight_load.wait()
    pltpu.make_async_copy(att_in, att_in, att_recv).wait()
    head_rows = att_in[...].reshape(seqs, head_dim).astype(jnp.bfloat16)
    for dz in range(SIDE):
        base = pl.multiple_of(dz * chunk, chunk)
        partial = jnp.dot(
            head_rows, out_weight_buf[:, pl.ds(base, chunk)], preferred_element_type=jnp.float32
        ).astype(jnp.bfloat16)
        for j in range(chunk_blocks):
            part_out[dz * chunk_blocks + j] = partial[:, j * LANES : (j + 1) * LANES]
    for step in CUBE_STEPS:
        target = at(*step)
        src = part_out.at[target // 2]
        dst = part_in.at[d]
        if step == (0, 0, 0):
            pltpu.make_async_copy(src, dst, part_recv).start()
        else:
            pltpu.make_async_remote_copy(
                src, dst, part_send, part_recv, device_id=(s, target), device_id_type=MESH
            ).start()

    my_block = d // 2
    my_half = lax.rem(d, 2)
    lanes_at = pl.multiple_of(my_block * LANES, LANES)
    hidden_load.wait()
    gain_load.wait()
    hidden_block = hidden_ref[:, pl.ds(lanes_at, LANES)].astype(jnp.float32)
    gain = gain_ref[...].astype(jnp.float32)
    gain_buf[...] = gain
    inverse_buf[...] = 1.0 / (gain * gain)
    gain_block = gain_buf[pl.ds(my_block, 1), :]

    pltpu.make_async_copy(part_in, part_in, part_recv).wait()
    residual = hidden_block
    for i in range(part_in.shape[0]):
        residual = residual + part_in[i].astype(jnp.float32)
    block_out[...] = (residual * gain_block).astype(jnp.bfloat16)

    for step in CUBE_STEPS:
        dst = rows_in.at[my_block, s]

        def send_block(dst=dst, target=at(*step), dz=step[0]):
            pltpu.make_async_remote_copy(
                block_out,
                dst,
                rows_send,
                rows_recv.at[dz],
                device_id=(my_half, target),
                device_id_type=MESH,
            ).start()

        if step == (0, 0, 0):
            pl.when(my_half != s)(send_block)

            @pl.when(my_half == s)
            def _():
                pltpu.make_async_copy(block_out, dst, rows_recv.at[0]).start()
        else:
            send_block()

    gate_proj = jnp.zeros((2 * CAP, gate_buf.shape[1]), jnp.float32)
    up_proj = jnp.zeros((2 * CAP, gate_buf.shape[1]), jnp.float32)
    squares = jnp.zeros((2 * CAP, LANES), jnp.float32)
    gate_load.wait()
    up_load.wait()
    for dz in (0, 1, 3, 2):
        plane = lax.rem(z + SIDE - dz, SIDE)
        arrived = rows_in.at[pl.ds(plane * chunk_blocks, chunk_blocks)]
        pltpu.make_async_copy(arrived, arrived, rows_recv.at[dz]).wait()
        tokens = jnp.concatenate(
            [rows_in[plane * chunk_blocks + j].reshape(rows, LANES) for j in range(chunk_blocks)],
            axis=1,
        )
        picked_rows = jnp.dot(pick, tokens, preferred_element_type=jnp.float32)
        tokens = picked_rows.astype(jnp.bfloat16)
        base = pl.multiple_of(plane * chunk, chunk)
        gate_proj = gate_proj + jnp.dot(
            tokens, gate_buf[pl.ds(base, chunk), :], preferred_element_type=jnp.float32
        )
        up_proj = up_proj + jnp.dot(
            tokens, up_buf[pl.ds(base, chunk), :], preferred_element_type=jnp.float32
        )
        for j in range(chunk_blocks):
            wide = picked_rows[:, j * LANES : (j + 1) * LANES]
            row = plane * chunk_blocks + j
            squares = squares + wide * wide * inverse_buf[pl.ds(row, 1), :]
    scale = lax.rsqrt(jnp.sum(squares, axis=1, keepdims=True) / width + NORM_EPS)
    gate_proj = gate_proj * scale
    up_proj = up_proj * scale
    packed = (gate_proj * jax.nn.sigmoid(gate_proj) * up_proj).astype(jnp.bfloat16)

    down_load.wait()
    low_lane = lax.broadcasted_iota(jnp.int32, (CAP, LANES), 1) < LANES // 2

    def down():
        product = jnp.dot(packed, down_buf[...], preferred_element_type=jnp.float32)
        for j in range(chunk_blocks * SIDE):
            block = product[:, j * LANES : (j + 1) * LANES]
            turned = pltpu.roll(block, LANES // 2, 1)
            pair = (
                jnp.where(low_lane, block[:CAP], turned[CAP:]),
                jnp.where(low_lane, turned[:CAP], block[CAP:]),
            )
            for half in range(2):
                owner = j * 2 + half
                for batch in range(2):
                    comb_out[owner, batch] = pair[half][2 * batch : 2 * batch + 2]

    def combine(order):
        dz = RING_ORDER[order]
        for dx, dy in PLANE_STEPS:
            target = at(dz, dx, dy)
            dst = comb_in.at[s, d]
            for batch in (1, 0):
                src = comb_out.at[target, batch]
                if (dz, dx, dy, batch) == (0, 0, 0, 0):
                    pltpu.make_async_copy(src, dst, comb_recv).start()
                else:
                    group = s if batch == 0 else 1 - s
                    pltpu.make_async_remote_copy(
                        src, dst, comb_send, comb_recv, device_id=(group, target), device_id_type=MESH
                    ).start()

    down()
    for step in CUBE_STEPS:
        target = at(*step)
        dst = comb_in.at[s, d]
        for batch in (1, 0):
            src = comb_out.at[target, batch]
            if step == (0, 0, 0) and batch == 0:
                pltpu.make_async_copy(src, dst, comb_recv).start()
            else:
                group = s if batch == 0 else 1 - s
                pltpu.make_async_remote_copy(
                    src, dst, comb_send, comb_recv, device_id=(group, target), device_id_type=MESH
                ).start()

    router_load.wait()
    own_tokens = jnp.concatenate([rows_in[k, s] for k in range(rows_in.shape[0])], axis=1)
    own_squares = jnp.zeros((seqs, LANES), jnp.float32)
    for k in range(rows_in.shape[0]):
        wide = rows_in[k, s].astype(jnp.float32)
        own_squares = own_squares + wide * wide * inverse_buf[k : k + 1, :]
    own_scale = lax.rsqrt(jnp.sum(own_squares, axis=1, keepdims=True) / width + NORM_EPS)
    logits = lax.dot_general(
        own_tokens, router_buf[...], (((1,), (1,)), ((), ())), preferred_element_type=jnp.float32
    )
    shares = match * jax.nn.sigmoid(logits * own_scale)
    gates = shares / jnp.sum(shares, axis=1, keepdims=True)
    gate_slots = jnp.dot(
        gates, spread, precision=lax.Precision.HIGHEST, preferred_element_type=jnp.float32
    )
    gate_slots = jnp.where(in_slot, jnp.concatenate([gate_slots, gate_slots], axis=0), 0.0)

    pltpu.make_async_copy(comb_in, comb_in, comb_recv).wait()
    expert_rows = (comb_in[0] + comb_in[1]).reshape(slots, LANES)
    routed = jnp.dot(
        gate_slots,
        expert_rows,
        precision=lax.Precision.HIGHEST,
        preferred_element_type=jnp.float32,
    )
    features = out_ref.shape[2]
    mixed = jnp.where(my_half == 0, residual[:, :features], residual[:, features:])
    mixed = mixed + routed[:seqs, :features] + routed[seqs:, features:]
    out_ref[0] = mixed.astype(out_ref.dtype)

    most = att_in.at[pl.ds(0, PLANE - 1)]
    pltpu.make_async_copy(most, most, att_send).wait()

    @pl.when(y != z)
    def _():
        pltpu.make_async_copy(att_in.at[0], att_in.at[0], att_send).wait()

    most = part_in.at[pl.ds(0, SIDE * PLANE - 1)]
    pltpu.make_async_copy(most, most, part_send).wait()
    pltpu.make_async_copy(most, most, rows_send).wait()

    @pl.when(my_half != s)
    def _():
        pltpu.make_async_copy(block_out, block_out, rows_send).wait()

    pltpu.make_async_copy(comb_in.at[0], comb_in.at[0], comb_send).wait()
    most = comb_in.at[0, pl.ds(0, SIDE * PLANE - 1)]
    pltpu.make_async_copy(most, most, comb_send).wait()


def body(
    hidden_in,
    queries,
    key_cache,
    value_cache,
    kv_lengths,
    route_ids,
    out_weight,
    norm_gain,
    router_weight,
    w_gate,
    w_up,
    w_down,
):
    seqs, width = hidden_in.shape[1:]
    kv_span, head_dim = key_cache.shape[2:]
    experts = router_weight.shape[1]
    hidden_units = w_gate.shape[2]
    devices = lax.axis_size("dev")
    blocks = width // LANES
    vmem = pl.BlockSpec(memory_space=pltpu.VMEM)
    dma = pltpu.SemaphoreType.DMA
    return pl.pallas_call(
        layer_kernel,
        out_shape=jax.ShapeDtypeStruct((1, seqs, width // devices), jnp.bfloat16),
        in_specs=[pl.BlockSpec(memory_space=pl.ANY)] * 12,
        out_specs=vmem,
        scratch_shapes=[
            pltpu.VMEM((seqs, width), jnp.bfloat16),
            pltpu.VMEM(queries.shape[2:], jnp.bfloat16),
            pltpu.SMEM(kv_lengths.shape, jnp.int32),
            pltpu.VMEM((2, route_ids.shape[2], seqs), jnp.int32),
            pltpu.VMEM((blocks, LANES), jnp.bfloat16),
            pltpu.VMEM((kv_span, head_dim), jnp.bfloat16),
            pltpu.VMEM((kv_span, head_dim), jnp.bfloat16),
            pltpu.VMEM(out_weight.shape, jnp.bfloat16),
            pltpu.VMEM((experts, width), jnp.bfloat16),
            pltpu.VMEM((width, hidden_units), jnp.bfloat16),
            pltpu.VMEM((width, hidden_units), jnp.bfloat16),
            pltpu.VMEM((hidden_units, width), jnp.bfloat16),
            pltpu.VMEM((seqs, 1, head_dim), jnp.float32),
            pltpu.VMEM((seqs, 1, head_dim), jnp.float32),
            pltpu.VMEM((blocks, seqs, LANES), jnp.bfloat16),
            pltpu.VMEM((devices, seqs, LANES), jnp.bfloat16),
            pltpu.VMEM((seqs, LANES), jnp.bfloat16),
            pltpu.VMEM((blocks, 2, seqs, LANES), jnp.bfloat16),
            pltpu.VMEM((blocks, LANES), jnp.float32),
            pltpu.VMEM((blocks, LANES), jnp.float32),
            pltpu.VMEM((devices, 2, CAP // 2, LANES), jnp.float32),
            pltpu.VMEM((2, devices, CAP // 2, LANES), jnp.float32),
            dma((12,)),
            dma,
            dma,
            dma,
            dma,
            dma,
            dma((SIDE,)),
            dma,
            dma,
        ],
        compiler_params=pltpu.CompilerParams(
            collective_id=0, has_side_effects=True, vmem_limit_bytes=32 * 2**20
        ),
    )(*[
        pltpu.with_memory_space_constraint(operand, pltpu.HBM) for operand in (
        hidden_in,
        queries,
        key_cache,
        value_cache,
        kv_lengths,
        jnp.swapaxes(route_ids, 1, 2),
        out_weight,
        norm_gain.reshape(blocks, LANES),
        router_weight.T,
        w_gate,
        w_up,
        w_down,
    )])


def solution(mesh):
    placed = (
        P("sec", None, None),
        P("sec", "dev", None, None),
        P("sec", "dev", None, None),
        P("sec", "dev", None, None),
        P("sec", None),
        P(),
        P("dev", None),
        P(),
        P(),
        P("dev", None, "sec"),
        P("dev", None, "sec"),
        P("dev", "sec", None),
    )
    return jax.shard_map(
        body, mesh=mesh, in_specs=placed, out_specs=P("sec", None, "dev"), check_vma=False
    )
```

```python
import functools

import jax
import jax.numpy as jnp
from jax import lax
from jax.experimental import pallas as pl
from jax.experimental.pallas import tpu as pltpu
from jax.sharding import PartitionSpec as P

MASKED_SCORE = -1e30
NORM_EPS = 1e-06
MESH = pl.DeviceIdType.MESH
LANES = 128
CAP = 4
SIDE = 4
PLANE = SIDE * SIDE
RING_ORDER = (2, 1, 3, 0)


def hops(step):
    return min(step, SIDE - step)


def far_first(steps):
    return sorted(steps, key=lambda step: -sum(hops(part) for part in step))


PLANE_STEPS = far_first([(dx, dy) for dx in range(SIDE) for dy in range(SIDE)])
CUBE_STEPS = far_first(
    [(dz, dx, dy) for dz in range(SIDE) for dx in range(SIDE) for dy in range(SIDE)]
)


def layer_kernel(
    hidden_hbm,
    query_hbm,
    key_hbm,
    value_hbm,
    length_hbm,
    route_hbm,
    out_weight_hbm,
    gain_hbm,
    router_hbm,
    gate_hbm,
    up_hbm,
    down_hbm,
    out_ref,
    hidden_ref,
    query_ref,
    length_ref,
    route_ref,
    gain_ref,
    key_buf,
    value_buf,
    out_weight_buf,
    router_buf,
    gate_buf,
    up_buf,
    down_buf,
    att_out,
    att_in,
    part_out,
    part_in,
    block_out,
    rows_in,
    gain_buf,
    inverse_buf,
    comb_out,
    comb_in,
    load_sem,
    att_send,
    att_recv,
    part_send,
    part_recv,
    rows_send,
    rows_recv,
    comb_send,
    comb_recv,
):
    s = lax.axis_index("sec")
    d = lax.axis_index("dev")
    z = d // PLANE
    x = lax.rem(d // SIDE, SIDE)
    y = lax.rem(d, SIDE)
    seqs = hidden_ref.shape[0]
    kv_span = key_buf.shape[0]
    head_dim = key_buf.shape[1]
    width = out_weight_buf.shape[1]
    rows = 2 * seqs
    chunk = width // SIDE
    chunk_blocks = chunk // LANES

    loads = [
        pltpu.make_async_copy(src, dst, load_sem.at[i])
        for i, (src, dst) in enumerate(
            (
                (length_hbm, length_ref),
                (query_hbm.at[0, 0], query_ref),
                (key_hbm.at[0, 0], key_buf),
                (value_hbm.at[0, 0], value_buf),
                (route_hbm, route_ref),
                (out_weight_hbm, out_weight_buf),
                (gate_hbm.at[0], gate_buf),
                (up_hbm.at[0], up_buf),
                (router_hbm, router_buf),
                (down_hbm.at[0], down_buf),
                (hidden_hbm.at[0], hidden_ref),
                (gain_hbm, gain_ref),
            )
        )
    ]
    (
        length_load,
        query_load,
        key_load,
        value_load,
        route_load,
        out_weight_load,
        gate_load,
        up_load,
        router_load,
        down_load,
        hidden_load,
        gain_load,
    ) = loads
    zs = [lax.rem(z + i, SIDE) for i in range(SIDE)]
    xs = [lax.rem(x + i, SIDE) for i in range(SIDE)]
    ys = [lax.rem(y + i, SIDE) for i in range(SIDE)]

    def at(dz, dx, dy):
        return zs[dz] * PLANE + xs[dx] * SIDE + ys[dy]

    barrier = pltpu.get_barrier_semaphore()

    def greet(target):
        pl.semaphore_signal(barrier, inc=1, device_id=(s, target), device_id_type=MESH)

    for load in loads[:4]:
        load.start()
    pl.semaphore_signal(barrier, inc=1, device_id=(1 - s, d), device_id_type=MESH)
    for dz, dx in PLANE_STEPS[:-1]:
        greet(zs[dz] * PLANE + xs[dx] * SIDE + z)
    for dx, turn in PLANE_STEPS:
        if turn:
            greet(y * PLANE + xs[dx] * SIDE + zs[turn])
    pl.when(y != z)(lambda: greet(z * PLANE + x * SIDE + z))
    for load in loads[4:]:
        load.start()

    query_load.wait()
    length_load.wait()
    key_load.wait()
    scores = lax.dot_general(
        query_ref[...], key_buf[...], (((1,), (1,)), ((), ())), preferred_element_type=jnp.float32
    ) * head_dim ** (-0.5)
    length = length_ref[0, d // SIDE]
    is_valid = lax.broadcasted_iota(jnp.int32, scores.shape, 1) < length
    scores = jnp.where(is_valid, scores, MASKED_SCORE)
    top = jnp.max(scores, axis=-1, keepdims=True)
    weights = jnp.where(is_valid, jnp.exp(scores - top), 0.0).astype(jnp.bfloat16)
    total = jnp.sum(weights.astype(jnp.float32), axis=-1, keepdims=True)
    value_load.wait()
    attended = jnp.dot(weights, value_buf[...], preferred_element_type=jnp.float32) / total
    att_out[...] = attended.reshape(att_out.shape)

    pl.semaphore_wait(barrier, 2 * PLANE - SIDE + 1 - (y == z).astype(jnp.int32))
    seq = d // SIDE
    for dx, dy in PLANE_STEPS:
        in_plane = xs[dx] * SIDE + ys[dy]
        src = att_out.at[in_plane]
        dst = att_in.at[seq]

        def send_row(src=src, dst=dst, target=y * PLANE + in_plane):
            pltpu.make_async_remote_copy(
                src, dst, att_send, att_recv, device_id=(s, target), device_id_type=MESH
            ).start()

        if (dx, dy) == (0, 0):
            pl.when(y != z)(send_row)

            @pl.when(y == z)
            def _():
                pltpu.make_async_copy(src, dst, att_recv).start()
        else:
            send_row()

    experts = router_buf.shape[0]
    route_load.wait()

    def match_of(routes):
        expert_row = lax.broadcasted_iota(jnp.int32, (experts, routes.shape[1]), 0)
        match = jnp.zeros(expert_row.shape, jnp.float32)
        for k in range(routes.shape[0]):
            match = match + (routes[k : k + 1] == expert_row).astype(jnp.float32)
        return match.astype(jnp.bfloat16)

    def exact_dot(left, right, left_dim=1, right_dim=0):
        return lax.dot_general(
            left.astype(jnp.bfloat16),
            right.astype(jnp.bfloat16),
            (((left_dim,), (right_dim,)), ((), ())),
            preferred_element_type=jnp.float32,
        )

    def iota(shape, dim):
        return lax.broadcasted_iota(jnp.int32, shape, dim)

    routes = jnp.concatenate([route_ref[0], route_ref[1]], axis=1)
    chosen_row = jnp.sum((routes == d).astype(jnp.float32), axis=0, keepdims=True)
    row_a, row_b = iota((rows, rows), 0), iota((rows, rows), 1)
    before = (row_a < row_b) & (row_a // seqs == row_b // seqs)
    rank_row = exact_dot(jnp.broadcast_to(chosen_row, (2 * CAP, rows)), before)
    slot, token = iota((2 * CAP, rows), 0), iota((2 * CAP, rows), 1)
    pick = (
        (token // seqs == slot // CAP)
        & (rank_row == lax.rem(slot, CAP).astype(jnp.float32))
        & (chosen_row > 0.5)
    )
    chosen = exact_dot(pick, match_of(routes), 1, 1)

    match_rows = match_of(route_ref[s])
    token_a, token_b = iota((seqs, seqs), 0), iota((seqs, seqs), 1)
    rank_rows = exact_dot(match_rows, token_a < token_b)
    wide = experts * CAP
    to_slots = iota((wide, experts), 0) // CAP == iota((wide, experts), 1)
    gather_rows = (exact_dot(to_slots, match_rows) > 0.5) & (
        exact_dot(to_slots, rank_rows) == lax.rem(iota((wide, seqs), 0), CAP).astype(jnp.float32)
    )
    match = exact_dot(token_a == token_b, match_rows, 1, 1)
    rank = exact_dot(token_a == token_b, rank_rows, 1, 1)
    slots = experts * 2
    spread = iota((experts, slots), 1) // 2 == iota((experts, slots), 0)
    match_slots = exact_dot(match, spread) > 0.5
    rank_slots = exact_dot(rank, spread)
    low_slot = lax.rem(iota((seqs, slots), 1), 2).astype(jnp.float32)
    scatter_rows = jnp.concatenate(
        [
            jnp.where(match_slots & (rank_slots == low_slot + 2.0 * i), 1.0, 0.0)
            for i in range(CAP // 2)
        ],
        axis=0,
    )

    out_weight_load.wait()
    pltpu.make_async_copy(att_in, att_in, att_recv).wait()
    head_rows = att_in[...].reshape(seqs, head_dim).astype(jnp.bfloat16)
    for dz in range(SIDE):
        base = pl.multiple_of(dz * chunk, chunk)
        partial = jnp.dot(
            head_rows, out_weight_buf[:, pl.ds(base, chunk)], preferred_element_type=jnp.float32
        ).astype(jnp.bfloat16)
        for j in range(chunk_blocks):
            part_out[dz * chunk_blocks + j] = partial[:, j * LANES : (j + 1) * LANES]
    for step in CUBE_STEPS:
        target = at(*step)
        src = part_out.at[target // 2]
        dst = part_in.at[d]
        if step == (0, 0, 0):
            pltpu.make_async_copy(src, dst, part_recv).start()
        else:
            pltpu.make_async_remote_copy(
                src, dst, part_send, part_recv, device_id=(s, target), device_id_type=MESH
            ).start()

    my_block = d // 2
    my_half = lax.rem(d, 2)
    lanes_at = pl.multiple_of(my_block * LANES, LANES)
    hidden_load.wait()
    gain_load.wait()
    hidden_block = hidden_ref[:, pl.ds(lanes_at, LANES)].astype(jnp.float32)
    gain = gain_ref[...].astype(jnp.float32)
    gain_buf[...] = gain
    inverse_buf[...] = 1.0 / (gain * gain)
    gain_block = gain_buf[pl.ds(my_block, 1), :]

    pltpu.make_async_copy(part_in, part_in, part_recv).wait()
    residual = hidden_block
    for i in range(part_in.shape[0]):
        residual = residual + part_in[i].astype(jnp.float32)
    block = (residual * gain_block).astype(jnp.bfloat16)
    block_rows = exact_dot(gather_rows, block)
    for e in range(experts):
        block_out[e] = block_rows[e * CAP : (e + 1) * CAP]

    for step in CUBE_STEPS:
        src = block_out.at[at(*step)]
        dst = rows_in.at[my_block, s]

        def send_block(src=src, dst=dst, target=at(*step), dz=step[0]):
            pltpu.make_async_remote_copy(
                src,
                dst,
                rows_send,
                rows_recv.at[dz],
                device_id=(my_half, target),
                device_id_type=MESH,
            ).start()

        if step == (0, 0, 0):
            pl.when(my_half != s)(send_block)

            @pl.when(my_half == s)
            def _():
                pltpu.make_async_copy(src, dst, rows_recv.at[0]).start()
        else:
            send_block()

    gate_proj = jnp.zeros((2 * CAP, gate_buf.shape[1]), jnp.float32)
    up_proj = jnp.zeros((2 * CAP, gate_buf.shape[1]), jnp.float32)
    squares = jnp.zeros((2 * CAP, LANES), jnp.float32)
    logits = jnp.zeros((2 * CAP, experts), jnp.float32)
    router_load.wait()
    gate_load.wait()
    up_load.wait()
    for dz in (0, 1, 3, 2):
        plane = lax.rem(z + SIDE - dz, SIDE)
        arrived = rows_in.at[pl.ds(plane * chunk_blocks, chunk_blocks)]
        pltpu.make_async_copy(arrived, arrived, rows_recv.at[dz]).wait()
        picked_rows = jnp.concatenate(
            [
                rows_in[plane * chunk_blocks + j].reshape(2 * CAP, LANES)
                for j in range(chunk_blocks)
            ],
            axis=1,
        )
        tokens = picked_rows.astype(jnp.bfloat16)
        base = pl.multiple_of(plane * chunk, chunk)
        gate_proj = gate_proj + jnp.dot(
            tokens, gate_buf[pl.ds(base, chunk), :], preferred_element_type=jnp.float32
        )
        up_proj = up_proj + jnp.dot(
            tokens, up_buf[pl.ds(base, chunk), :], preferred_element_type=jnp.float32
        )
        logits = logits + lax.dot_general(
            tokens,
            router_buf[:, pl.ds(base, chunk)],
            (((1,), (1,)), ((), ())),
            preferred_element_type=jnp.float32,
        )
        for j in range(chunk_blocks):
            wide = picked_rows[:, j * LANES : (j + 1) * LANES]
            row = plane * chunk_blocks + j
            squares = squares + wide * wide * inverse_buf[pl.ds(row, 1), :]
    scale = lax.rsqrt(jnp.sum(squares, axis=1, keepdims=True) / width + NORM_EPS)
    shares = chosen * jax.nn.sigmoid(logits * scale)
    share_sum = jnp.sum(shares, axis=1, keepdims=True)
    own_share = jnp.sum(
        jnp.where(iota(shares.shape, 1) == d, shares, 0.0), axis=1, keepdims=True
    )
    gates = jnp.where(share_sum > 0.0, own_share / share_sum, 0.0)
    gate_proj = gate_proj * scale
    up_proj = up_proj * scale
    packed = (gate_proj * jax.nn.sigmoid(gate_proj) * up_proj).astype(jnp.bfloat16)

    down_load.wait()
    low_lane = iota((CAP // 2, LANES), 1) < LANES // 2

    def down(plane):
        product = gates * jnp.dot(
            packed,
            down_buf[:, plane * chunk : (plane + 1) * chunk],
            preferred_element_type=jnp.float32,
        )
        for j in range(chunk_blocks):
            block = product[:, j * LANES : (j + 1) * LANES]
            turned = pltpu.roll(block, LANES // 2, 1)
            owner = plane * PLANE + j * 2
            for batch in range(2):
                low = slice(batch * CAP, batch * CAP + CAP // 2)
                high = slice(batch * CAP + CAP // 2, (batch + 1) * CAP)
                comb_out[owner, batch] = jnp.where(low_lane, block[low], turned[high])
                comb_out[owner + 1, batch] = jnp.where(low_lane, turned[low], block[high])

    def combine(plane):
        for dx, dy in PLANE_STEPS:
            target = plane * PLANE + xs[dx] * SIDE + ys[dy]
            dst = comb_in.at[s, d]
            for group in (1 - s, s):
                src = comb_out.at[target, group]

                def send_rows(src=src, dst=dst, group=group, target=target):
                    pltpu.make_async_remote_copy(
                        src, dst, comb_send, comb_recv, device_id=(group, target), device_id_type=MESH
                    ).start()

                if (dx, dy) == (0, 0) and group is s:
                    pl.when(z != plane)(send_rows)

                    @pl.when(z == plane)
                    def _(src=src, dst=dst):
                        pltpu.make_async_copy(src, dst, comb_recv).start()
                else:
                    send_rows()

    for plane in (0, 1, 3, 2):
        down(plane)
        combine(plane)

    pltpu.make_async_copy(comb_in, comb_in, comb_recv).wait()
    expert_rows = (comb_in[0] + comb_in[1]).reshape(slots, LANES)
    routed = jnp.dot(
        scatter_rows,
        expert_rows,
        precision=lax.Precision.HIGHEST,
        preferred_element_type=jnp.float32,
    )
    features = out_ref.shape[2]
    mixed = jnp.where(my_half == 0, residual[:, :features], residual[:, features:])
    mixed = mixed + routed[:seqs, :features] + routed[seqs:, features:]
    out_ref[0] = mixed.astype(out_ref.dtype)

    most = att_in.at[pl.ds(0, PLANE - 1)]
    pltpu.make_async_copy(most, most, att_send).wait()

    @pl.when(y != z)
    def _():
        pltpu.make_async_copy(att_in.at[0], att_in.at[0], att_send).wait()

    most = part_in.at[pl.ds(0, SIDE * PLANE - 1)]
    pltpu.make_async_copy(most, most, part_send).wait()
    most = block_out.at[pl.ds(0, SIDE * PLANE - 1)]
    pltpu.make_async_copy(most, most, rows_send).wait()

    @pl.when(my_half != s)
    def _():
        pltpu.make_async_copy(block_out.at[0], block_out.at[0], rows_send).wait()

    pltpu.make_async_copy(comb_in.at[0], comb_in.at[0], comb_send).wait()
    most = comb_in.at[0, pl.ds(0, SIDE * PLANE - 1)]
    pltpu.make_async_copy(most, most, comb_send).wait()


def body(
    hidden_in,
    queries,
    key_cache,
    value_cache,
    kv_lengths,
    route_ids,
    out_weight,
    norm_gain,
    router_weight,
    w_gate,
    w_up,
    w_down,
):
    seqs, width = hidden_in.shape[1:]
    kv_span, head_dim = key_cache.shape[2:]
    experts = router_weight.shape[1]
    hidden_units = w_gate.shape[2]
    devices = lax.axis_size("dev")
    blocks = width // LANES
    vmem = pl.BlockSpec(memory_space=pltpu.VMEM)
    dma = pltpu.SemaphoreType.DMA
    return pl.pallas_call(
        layer_kernel,
        out_shape=jax.ShapeDtypeStruct((1, seqs, width // devices), jnp.bfloat16),
        in_specs=[pl.BlockSpec(memory_space=pl.ANY)] * 12,
        out_specs=vmem,
        scratch_shapes=[
            pltpu.VMEM((seqs, width), jnp.bfloat16),
            pltpu.VMEM(queries.shape[2:], jnp.bfloat16),
            pltpu.SMEM(kv_lengths.shape, jnp.int32),
            pltpu.VMEM((2, route_ids.shape[2], seqs), jnp.int32),
            pltpu.VMEM((blocks, LANES), jnp.bfloat16),
            pltpu.VMEM((kv_span, head_dim), jnp.bfloat16),
            pltpu.VMEM((kv_span, head_dim), jnp.bfloat16),
            pltpu.VMEM(out_weight.shape, jnp.bfloat16),
            pltpu.VMEM((experts, width), jnp.bfloat16),
            pltpu.VMEM((width, hidden_units), jnp.bfloat16),
            pltpu.VMEM((width, hidden_units), jnp.bfloat16),
            pltpu.VMEM((hidden_units, width), jnp.bfloat16),
            pltpu.VMEM((seqs, 1, head_dim), jnp.float32),
            pltpu.VMEM((seqs, 1, head_dim), jnp.float32),
            pltpu.VMEM((blocks, seqs, LANES), jnp.bfloat16),
            pltpu.VMEM((devices, seqs, LANES), jnp.bfloat16),
            pltpu.VMEM((experts, CAP, LANES), jnp.float32),
            pltpu.VMEM((blocks, 2, CAP, LANES), jnp.float32),
            pltpu.VMEM((blocks, LANES), jnp.float32),
            pltpu.VMEM((blocks, LANES), jnp.float32),
            pltpu.VMEM((devices, 2, CAP // 2, LANES), jnp.float32),
            pltpu.VMEM((2, devices, CAP // 2, LANES), jnp.float32),
            dma((12,)),
            dma,
            dma,
            dma,
            dma,
            dma,
            dma((SIDE,)),
            dma,
            dma,
        ],
        compiler_params=pltpu.CompilerParams(
            collective_id=0, has_side_effects=True, vmem_limit_bytes=32 * 2**20
        ),
    )(*[
        pltpu.with_memory_space_constraint(operand, pltpu.HBM) for operand in (
        hidden_in,
        queries,
        key_cache,
        value_cache,
        kv_lengths,
        jnp.swapaxes(route_ids, 1, 2),
        out_weight,
        norm_gain.reshape(blocks, LANES),
        router_weight.T,
        w_gate,
        w_up,
        w_down,
    )])


def solution(mesh):
    placed = (
        P("sec", None, None),
        P("sec", "dev", None, None),
        P("sec", "dev", None, None),
        P("sec", "dev", None, None),
        P("sec", None),
        P(),
        P("dev", None),
        P(),
        P(),
        P("dev", None, "sec"),
        P("dev", None, "sec"),
        P("dev", "sec", None),
    )
    return jax.shard_map(
        body, mesh=mesh, in_specs=placed, out_specs=P("sec", None, "dev"), check_vma=False
    )
```

```python
import jax
import jax.numpy as jnp
from jax import lax
from jax.experimental import pallas as pl
from jax.experimental.pallas import tpu as pltpu
from jax.sharding import PartitionSpec as P

MASKED_SCORE = -1e30
NORM_EPS = 1e-06
MESH = pl.DeviceIdType.MESH
LANES = 128
CAP = 4
SIDE = 4
PLANE = SIDE * SIDE
BATCH = 4


def hops(step):
    return min(step, SIDE - step)


def far_first(steps):
    return sorted(steps, key=lambda step: -sum(hops(part) for part in step))


PLANE_STEPS = far_first([(dx, dy) for dx in range(SIDE) for dy in range(SIDE)])
CUBE_STEPS = far_first(
    [(dz, dx, dy) for dz in range(SIDE) for dx in range(SIDE) for dy in range(SIDE)]
)

NEAR_STEPS = [
    (dz, dx, dy)
    for dz, dx, dy in CUBE_STEPS[::-1]
    if hops(dz) + hops(dx) + hops(dy) < hops((dz + 2) % 4) + hops((dx + 2) % 4) + hops((dy + 3) % 4)
]


def layer_kernel(
    hidden_hbm,
    query_hbm,
    key_hbm,
    value_hbm,
    length_hbm,
    route_hbm,
    out_weight_hbm,
    gain_hbm,
    router_hbm,
    gate_hbm,
    up_hbm,
    down_hbm,
    out_ref,
    hidden_ref,
    query_ref,
    length_ref,
    route_ref,
    gain_ref,
    key_buf,
    value_buf,
    out_weight_buf,
    router_buf,
    gate_buf,
    up_buf,
    down_buf,
    att_out,
    att_in,
    part_out,
    part_in,
    block_out,
    rows_in,
    gain_buf,
    inverse_buf,
    res_out,
    res_in,
    comb_out,
    comb_in,
    load_sem,
    att_send,
    att_recv,
    part_send,
    part_recv,
    rows_send,
    rows_recv,
    res_send,
    res_recv,
    comb_send,
    comb_recv,
):
    s = lax.axis_index("sec")
    d = lax.axis_index("dev")
    z = d // PLANE
    x = lax.rem(d // SIDE, SIDE)
    y = lax.rem(d, SIDE)
    seqs = hidden_ref.shape[0]
    head_dim = key_buf.shape[1]
    width = out_weight_buf.shape[1]
    rows = 2 * seqs
    chunk = width // SIDE
    chunk_blocks = chunk // LANES

    loads = [
        pltpu.make_async_copy(src, dst, load_sem.at[i])
        for i, (src, dst) in enumerate(
            (
                (length_hbm, length_ref),
                (query_hbm.at[0, 0], query_ref),
                (key_hbm.at[0, 0], key_buf),
                (value_hbm.at[0, 0], value_buf),
                (route_hbm, route_ref),
                (out_weight_hbm, out_weight_buf),
                (gate_hbm.at[0], gate_buf),
                (up_hbm.at[0], up_buf),
                (router_hbm, router_buf),
                (down_hbm.at[0], down_buf),
                (hidden_hbm.at[0], hidden_ref),
                (gain_hbm, gain_ref),
            )
        )
    ]
    (
        length_load,
        query_load,
        key_load,
        value_load,
        route_load,
        out_weight_load,
        gate_load,
        up_load,
        router_load,
        down_load,
        hidden_load,
        gain_load,
    ) = loads
    zs = [lax.rem(z + i, SIDE) for i in range(SIDE)]
    xs = [lax.rem(x + i, SIDE) for i in range(SIDE)]
    ys = [lax.rem(y + i, SIDE) for i in range(SIDE)]

    def at(dz, dx, dy):
        return zs[dz] * PLANE + xs[dx] * SIDE + ys[dy]

    barrier = pltpu.get_barrier_semaphore()

    def greet(target):
        pl.semaphore_signal(barrier, inc=1, device_id=(s, target), device_id_type=MESH)

    for load in loads[:4]:
        load.start()
    pl.semaphore_signal(barrier, inc=1, device_id=(1 - s, d), device_id_type=MESH)
    for dz, dx in PLANE_STEPS[:-1]:
        greet(zs[dz] * PLANE + xs[dx] * SIDE + z)
    for dx, turn in PLANE_STEPS:
        if turn:
            greet(y * PLANE + xs[dx] * SIDE + zs[turn])
    pl.when(y != z)(lambda: greet(z * PLANE + x * SIDE + z))
    for load in loads[4:]:
        load.start()

    query_load.wait()
    length_load.wait()
    key_load.wait()
    scores = lax.dot_general(
        query_ref[...], key_buf[...], (((1,), (1,)), ((), ())), preferred_element_type=jnp.float32
    ) * head_dim ** (-0.5)
    length = length_ref[0, d // SIDE]
    is_valid = lax.broadcasted_iota(jnp.int32, scores.shape, 1) < length
    scores = jnp.where(is_valid, scores, MASKED_SCORE)
    top = jnp.max(scores, axis=-1, keepdims=True)
    weights = jnp.where(is_valid, jnp.exp(scores - top), 0.0).astype(jnp.bfloat16)
    total = jnp.sum(weights.astype(jnp.float32), axis=-1, keepdims=True)
    value_load.wait()
    attended = jnp.dot(weights, value_buf[...], preferred_element_type=jnp.float32) / total
    att_out[...] = attended.reshape(att_out.shape)

    pl.semaphore_wait(barrier, 2 * PLANE - SIDE + 1 - (y == z).astype(jnp.int32))
    seq = d // SIDE
    for dx, dy in PLANE_STEPS:
        in_plane = xs[dx] * SIDE + ys[dy]
        src = att_out.at[in_plane]
        dst = att_in.at[seq]

        def send_row(src=src, dst=dst, target=y * PLANE + in_plane):
            pltpu.make_async_remote_copy(
                src, dst, att_send, att_recv, device_id=(s, target), device_id_type=MESH
            ).start()

        if (dx, dy) == (0, 0):
            pl.when(y != z)(send_row)

            @pl.when(y == z)
            def _():
                pltpu.make_async_copy(src, dst, att_recv).start()
        else:
            send_row()

    experts = router_buf.shape[0]
    route_load.wait()

    def match_of(routes):
        expert_row = lax.broadcasted_iota(jnp.int32, (experts, routes.shape[1]), 0)
        match = jnp.zeros(expert_row.shape, jnp.float32)
        for k in range(routes.shape[0]):
            match = match + (routes[k : k + 1] == expert_row).astype(jnp.float32)
        return match.astype(jnp.bfloat16)

    def exact_dot(left, right, left_dim=1, right_dim=0):
        return lax.dot_general(
            left.astype(jnp.bfloat16),
            right.astype(jnp.bfloat16),
            (((left_dim,), (right_dim,)), ((), ())),
            preferred_element_type=jnp.float32,
        )

    def iota(shape, dim):
        return lax.broadcasted_iota(jnp.int32, shape, dim)

    routes = jnp.concatenate([route_ref[0], route_ref[1]], axis=1)
    chosen_row = jnp.sum((routes == d).astype(jnp.float32), axis=0, keepdims=True)
    row_a, row_b = iota((rows, rows), 0), iota((rows, rows), 1)
    before = (row_a < row_b) & (row_a // seqs == row_b // seqs)
    rank_row = exact_dot(jnp.broadcast_to(chosen_row, (2 * CAP, rows)), before)
    slot, token = iota((2 * CAP, rows), 0), iota((2 * CAP, rows), 1)
    pick = (
        (token // seqs == slot // CAP)
        & (rank_row == lax.rem(slot, CAP).astype(jnp.float32))
        & (chosen_row > 0.5)
    )
    chosen = exact_dot(pick, match_of(routes), 1, 1)

    match_rows = match_of(route_ref[s])
    token_a, token_b = iota((seqs, seqs), 0), iota((seqs, seqs), 1)
    rank_rows = exact_dot(match_rows, token_a < token_b)
    wide = experts * CAP
    to_slots = iota((wide, experts), 0) // CAP == iota((wide, experts), 1)
    gather_rows = (exact_dot(to_slots, match_rows) > 0.5) & (
        exact_dot(to_slots, rank_rows) == lax.rem(iota((wide, seqs), 0), CAP).astype(jnp.float32)
    )
    match = exact_dot(token_a == token_b, match_rows, 1, 1)
    rank = exact_dot(token_a == token_b, rank_rows, 1, 1)
    slots = experts * 2
    spread = iota((experts, slots), 1) // 2 == iota((experts, slots), 0)
    match_slots = exact_dot(match, spread) > 0.5
    rank_slots = exact_dot(rank, spread)
    low_slot = lax.rem(iota((seqs, slots), 1), 2).astype(jnp.float32)
    scatter_rows = jnp.concatenate(
        [
            jnp.where(match_slots & (rank_slots == low_slot + 2.0 * i), 1.0, 0.0)
            for i in range(CAP // 2)
        ],
        axis=0,
    )

    out_weight_load.wait()
    pltpu.make_async_copy(att_in, att_in, att_recv).wait()
    head_rows = att_in[...].reshape(seqs, head_dim).astype(jnp.bfloat16)
    for dz in range(SIDE):
        base = pl.multiple_of(dz * chunk, chunk)
        partial = jnp.dot(
            head_rows, out_weight_buf[:, pl.ds(base, chunk)], preferred_element_type=jnp.float32
        ).astype(jnp.bfloat16)
        for j in range(chunk_blocks):
            part_out[dz * chunk_blocks + j] = partial[:, j * LANES : (j + 1) * LANES]
    odd = lax.rem(y, 2)
    shifts = (2 * odd, 2 * (1 - odd))
    block_z = [[lax.rem(z + i + shift, SIDE) for i in range(SIDE)] for shift in shifts]
    block_x = [[lax.rem(x + i + shift, SIDE) for i in range(SIDE)] for shift in shifts]

    def block_at(dz, dx, dy):
        place = block_z[dy % 2][dz] * SIDE + block_x[dy % 2][dx]
        return place * 2 + ys[dy] // 2

    for step in CUBE_STEPS:
        target = at(*step)
        src = part_out.at[block_at(*step)]
        dst = part_in.at[d]
        if step == (0, 0, 0):
            pltpu.make_async_copy(src, dst, part_recv).start()
        else:
            pltpu.make_async_remote_copy(
                src, dst, part_send, part_recv, device_id=(s, target), device_id_type=MESH
            ).start()

    my_block = block_at(0, 0, 0)
    lanes_at = pl.multiple_of(my_block * LANES, LANES)
    hidden_load.wait()
    gain_load.wait()
    hidden_block = hidden_ref[:, pl.ds(lanes_at, LANES)].astype(jnp.float32)
    gain = gain_ref[...].astype(jnp.float32)
    gain_buf[...] = gain
    inverse_buf[...] = 1.0 / (gain * gain)
    gain_block = gain_buf[pl.ds(my_block, 1), :]

    pltpu.make_async_copy(part_in, part_in, part_recv).wait()
    residual = hidden_block
    for i in range(part_in.shape[0]):
        residual = residual + part_in[i].astype(jnp.float32)
    block = (residual * gain_block).astype(jnp.bfloat16)
    block_rows = exact_dot(gather_rows, block)
    for e in range(experts):
        block_out[e] = block_rows[e * CAP : (e + 1) * CAP]

    turn = 1 - 2 * odd
    near_z = [lax.rem(z + turn * i + SIDE, SIDE) for i in range(SIDE)]
    near_x = [lax.rem(x + turn * i + SIDE, SIDE) for i in range(SIDE)]
    near_y = [lax.rem(y + turn * i + SIDE, SIDE) for i in range(SIDE)]
    for place, (dz, dx, dy) in enumerate(NEAR_STEPS):
        target = near_z[dz] * PLANE + near_x[dx] * SIDE + near_y[dy]
        src = block_out.at[target]
        dst = rows_in.at[place, s]
        arrival = rows_recv.at[place // BATCH]
        for group in (1 - s, s):
            if (dz, dx, dy) == (0, 0, 0) and group is s:
                pltpu.make_async_copy(src, dst, arrival).start()
            else:
                pltpu.make_async_remote_copy(
                    src, dst, rows_send, arrival, device_id=(group, target), device_id_type=MESH
                ).start()

    res_out[...] = residual
    res_copy = pltpu.make_async_remote_copy(
        res_out, res_in, res_send, res_recv, device_id=(s, d + turn), device_id_type=MESH
    )

    @pl.when(odd == 0)
    def _():
        res_in[...] = residual
        res_copy.start()

    gate_proj = jnp.zeros((2 * CAP, gate_buf.shape[1]), jnp.float32)
    up_proj = jnp.zeros((2 * CAP, gate_buf.shape[1]), jnp.float32)
    squares = jnp.zeros((2 * CAP, LANES), jnp.float32)
    logits = jnp.zeros((2 * CAP, experts), jnp.float32)
    router_load.wait()
    gate_load.wait()
    up_load.wait()
    def from_steps(center, shift, side):
        return [lax.rem(center + SIDE - (1 - 2 * side) * i + shift * side, SIDE) for i in range(SIDE)]

    sides = (odd, 1 - odd)
    from_z = [from_steps(z, 2, side) for side in sides]
    from_x = [from_steps(x, 2, side) for side in sides]
    from_y = [from_steps(y, 0, side) for side in sides]
    for place, (dz, dx, dy) in enumerate(NEAR_STEPS):
        if place % BATCH == 0:
            arrived = rows_in.at[pl.ds(place, BATCH)]
            pltpu.make_async_copy(arrived, arrived, rows_recv.at[place // BATCH]).wait()
        side = dy % 2
        row = (from_z[side][dz] * SIDE + from_x[side][dx]) * 2 + from_y[side][dy] // 2
        base = pl.multiple_of(row * LANES, LANES)
        picked_rows = rows_in[place].reshape(2 * CAP, LANES)
        tokens = picked_rows.astype(jnp.bfloat16)
        gate_proj = gate_proj + jnp.dot(
            tokens, gate_buf[pl.ds(base, LANES), :], preferred_element_type=jnp.float32
        )
        up_proj = up_proj + jnp.dot(
            tokens, up_buf[pl.ds(base, LANES), :], preferred_element_type=jnp.float32
        )
        logits = logits + lax.dot_general(
            tokens,
            router_buf[:, pl.ds(base, LANES)],
            (((1,), (1,)), ((), ())),
            preferred_element_type=jnp.float32,
        )
        squares = squares + picked_rows * picked_rows * inverse_buf[pl.ds(row, 1), :]
    scale = lax.rsqrt(jnp.sum(squares, axis=1, keepdims=True) / width + NORM_EPS)
    shares = chosen * jax.nn.sigmoid(logits * scale)
    share_sum = jnp.sum(shares, axis=1, keepdims=True)
    own_share = jnp.sum(
        jnp.where(iota(shares.shape, 1) == d, shares, 0.0), axis=1, keepdims=True
    )
    gates = jnp.where(share_sum > 0.0, own_share / share_sum, 0.0)
    gate_proj = gate_proj * scale
    up_proj = up_proj * scale
    packed = (gate_proj * jax.nn.sigmoid(gate_proj) * up_proj).astype(jnp.bfloat16)

    down_load.wait()
    low_lane = iota((CAP // 2, LANES), 1) < LANES // 2

    def down(plane):
        product = gates * jnp.dot(
            packed,
            down_buf[:, plane * chunk : (plane + 1) * chunk],
            preferred_element_type=jnp.float32,
        )
        for j in range(chunk_blocks):
            block = product[:, j * LANES : (j + 1) * LANES]
            turned = pltpu.roll(block, LANES // 2, 1)
            owner = plane * PLANE + j * 2
            for batch in range(2):
                low = slice(batch * CAP, batch * CAP + CAP // 2)
                high = slice(batch * CAP + CAP // 2, (batch + 1) * CAP)
                comb_out[owner, batch] = jnp.where(low_lane, block[low], turned[high])
                comb_out[owner + 1, batch] = jnp.where(low_lane, turned[low], block[high])

    def combine(plane):
        for dx, dy in PLANE_STEPS:
            target = plane * PLANE + xs[dx] * SIDE + ys[dy]
            dst = comb_in.at[s, d]
            for group in (1 - s, s):
                src = comb_out.at[target, group]

                def send_rows(src=src, dst=dst, group=group, target=target):
                    pltpu.make_async_remote_copy(
                        src, dst, comb_send, comb_recv, device_id=(group, target), device_id_type=MESH
                    ).start()

                if (dx, dy) == (0, 0) and group is s:
                    pl.when(z != plane)(send_rows)

                    @pl.when(z == plane)
                    def _(src=src, dst=dst):
                        pltpu.make_async_copy(src, dst, comb_recv).start()
                else:
                    send_rows()

    for plane in (0, 1, 3, 2):
        down(plane)
        combine(plane)

    pltpu.make_async_copy(comb_in, comb_in, comb_recv).wait()
    expert_rows = (comb_in[0] + comb_in[1]).reshape(slots, LANES)
    routed = jnp.dot(
        scatter_rows,
        expert_rows,
        precision=lax.Precision.HIGHEST,
        preferred_element_type=jnp.float32,
    )
    features = out_ref.shape[2]
    pl.when(odd == 1)(res_copy.wait_recv)
    residual = res_in[...]
    mixed = jnp.where(odd == 0, residual[:, :features], residual[:, features:])
    mixed = mixed + routed[:seqs, :features] + routed[seqs:, features:]
    out_ref[0] = mixed.astype(out_ref.dtype)

    most = att_in.at[pl.ds(0, PLANE - 1)]
    pltpu.make_async_copy(most, most, att_send).wait()

    @pl.when(y != z)
    def _():
        pltpu.make_async_copy(att_in.at[0], att_in.at[0], att_send).wait()

    most = part_in.at[pl.ds(0, SIDE * PLANE - 1)]
    pltpu.make_async_copy(most, most, part_send).wait()
    most = block_out.at[pl.ds(0, SIDE * PLANE - 1)]
    pltpu.make_async_copy(most, most, rows_send).wait()
    pl.when(odd == 0)(res_copy.wait_send)

    pltpu.make_async_copy(comb_in.at[0], comb_in.at[0], comb_send).wait()
    most = comb_in.at[0, pl.ds(0, SIDE * PLANE - 1)]
    pltpu.make_async_copy(most, most, comb_send).wait()


def body(
    hidden_in,
    queries,
    key_cache,
    value_cache,
    kv_lengths,
    route_ids,
    out_weight,
    norm_gain,
    router_weight,
    w_gate,
    w_up,
    w_down,
):
    seqs, width = hidden_in.shape[1:]
    kv_span, head_dim = key_cache.shape[2:]
    experts = router_weight.shape[1]
    hidden_units = w_gate.shape[2]
    devices = lax.axis_size("dev")
    blocks = width // LANES
    operands = (
        hidden_in,
        queries,
        key_cache,
        value_cache,
        kv_lengths,
        jnp.swapaxes(route_ids, 1, 2),
        out_weight,
        norm_gain.reshape(blocks, LANES),
        router_weight.T,
        w_gate,
        w_up,
        w_down,
    )
    dma = pltpu.SemaphoreType.DMA
    return pl.pallas_call(
        layer_kernel,
        out_shape=jax.ShapeDtypeStruct((1, seqs, width // devices), jnp.bfloat16),
        in_specs=[pl.BlockSpec(memory_space=pl.ANY)] * len(operands),
        out_specs=pl.BlockSpec(memory_space=pltpu.VMEM),
        scratch_shapes=[
            pltpu.VMEM((seqs, width), jnp.bfloat16),
            pltpu.VMEM(queries.shape[2:], jnp.bfloat16),
            pltpu.SMEM(kv_lengths.shape, jnp.int32),
            pltpu.VMEM((2, route_ids.shape[2], seqs), jnp.int32),
            pltpu.VMEM((blocks, LANES), jnp.bfloat16),
            pltpu.VMEM((kv_span, head_dim), jnp.bfloat16),
            pltpu.VMEM((kv_span, head_dim), jnp.bfloat16),
            pltpu.VMEM(out_weight.shape, jnp.bfloat16),
            pltpu.VMEM((experts, width), jnp.bfloat16),
            pltpu.VMEM((width, hidden_units), jnp.bfloat16),
            pltpu.VMEM((width, hidden_units), jnp.bfloat16),
            pltpu.VMEM((hidden_units, width), jnp.bfloat16),
            pltpu.VMEM((seqs, 1, head_dim), jnp.float32),
            pltpu.VMEM((seqs, 1, head_dim), jnp.float32),
            pltpu.VMEM((blocks, seqs, LANES), jnp.bfloat16),
            pltpu.VMEM((devices, seqs, LANES), jnp.bfloat16),
            pltpu.VMEM((experts, CAP, LANES), jnp.float32),
            pltpu.VMEM((blocks, 2, CAP, LANES), jnp.float32),
            pltpu.VMEM((blocks, LANES), jnp.float32),
            pltpu.VMEM((blocks, LANES), jnp.float32),
            pltpu.VMEM((seqs, LANES), jnp.float32),
            pltpu.VMEM((seqs, LANES), jnp.float32),
            pltpu.VMEM((devices, 2, CAP // 2, LANES), jnp.float32),
            pltpu.VMEM((2, devices, CAP // 2, LANES), jnp.float32),
            dma((12,)),
            dma,
            dma,
            dma,
            dma,
            dma,
            dma((blocks // BATCH,)),
            dma,
            dma,
            dma,
            dma,
        ],
        compiler_params=pltpu.CompilerParams(
            collective_id=0, has_side_effects=True, vmem_limit_bytes=32 * 2**20
        ),
    )(*[pltpu.with_memory_space_constraint(operand, pltpu.HBM) for operand in operands])


def solution(mesh):
    placed = (
        P("sec", None, None),
        P("sec", "dev", None, None),
        P("sec", "dev", None, None),
        P("sec", "dev", None, None),
        P("sec", None),
        P(),
        P("dev", None),
        P(),
        P(),
        P("dev", None, "sec"),
        P("dev", None, "sec"),
        P("dev", "sec", None),
    )
    return jax.shard_map(
        body, mesh=mesh, in_specs=placed, out_specs=P("sec", None, "dev"), check_vma=False
    )
```

```python
import jax
import jax.numpy as jnp
from jax import lax
from jax.experimental import pallas as pl
from jax.experimental.pallas import tpu as pltpu
from jax.sharding import PartitionSpec as P

MASKED_SCORE = -1e30
NORM_EPS = 1e-06
MESH = pl.DeviceIdType.MESH
LANES = 128
CAP = 4
SIDE = 4
PLANE = SIDE * SIDE
BATCH = 4


def hops(step):
    return min(step, SIDE - step)


def far_first(steps):
    return sorted(steps, key=lambda step: -sum(hops(part) for part in step))


PLANE_STEPS = far_first([(dx, dy) for dx in range(SIDE) for dy in range(SIDE)])
CUBE_STEPS = far_first(
    [(dz, dx, dy) for dz in range(SIDE) for dx in range(SIDE) for dy in range(SIDE)]
)

NEAR_STEPS = [
    (dz, dx, dy)
    for dz, dx, dy in CUBE_STEPS[::-1]
    if hops(dz) + hops(dx) + hops(dy) < hops((dz + 2) % 4) + hops((dx + 2) % 4) + hops((dy + 3) % 4)
]


def layer_kernel(
    hidden_hbm,
    query_hbm,
    key_hbm,
    value_hbm,
    length_hbm,
    route_hbm,
    out_weight_hbm,
    gain_hbm,
    router_hbm,
    gate_hbm,
    up_hbm,
    down_hbm,
    out_ref,
    hidden_ref,
    query_ref,
    length_ref,
    route_ref,
    gain_ref,
    key_buf,
    value_buf,
    out_weight_buf,
    router_buf,
    gate_buf,
    up_buf,
    down_buf,
    att_out,
    att_in,
    part_out,
    part_in,
    block_out,
    rows_in,
    gain_buf,
    inverse_buf,
    res_out,
    res_in,
    comb_out,
    comb_in,
    load_sem,
    att_send,
    att_recv,
    part_send,
    part_recv,
    rows_send,
    rows_recv,
    res_send,
    res_recv,
    comb_send,
    comb_recv,
):
    s = lax.axis_index("sec")
    d = lax.axis_index("dev")
    z = d // PLANE
    x = lax.rem(d // SIDE, SIDE)
    y = lax.rem(d, SIDE)
    seqs = hidden_ref.shape[0]
    head_dim = key_buf.shape[1]
    width = out_weight_buf.shape[1]
    rows = 2 * seqs
    chunk = width // SIDE
    chunk_blocks = chunk // LANES

    loads = [
        pltpu.make_async_copy(src, dst, load_sem.at[i])
        for i, (src, dst) in enumerate(
            (
                (length_hbm, length_ref),
                (query_hbm.at[0, 0], query_ref),
                (key_hbm.at[0, 0], key_buf),
                (value_hbm.at[0, 0], value_buf),
                (route_hbm, route_ref),
                (out_weight_hbm, out_weight_buf),
                (gate_hbm.at[0], gate_buf),
                (up_hbm.at[0], up_buf),
                (router_hbm, router_buf),
                (down_hbm.at[0], down_buf),
                (hidden_hbm.at[0], hidden_ref),
                (gain_hbm, gain_ref),
            )
        )
    ]
    (
        length_load,
        query_load,
        key_load,
        value_load,
        route_load,
        out_weight_load,
        gate_load,
        up_load,
        router_load,
        down_load,
        hidden_load,
        gain_load,
    ) = loads
    zs = [lax.rem(z + i, SIDE) for i in range(SIDE)]
    xs = [lax.rem(x + i, SIDE) for i in range(SIDE)]
    ys = [lax.rem(y + i, SIDE) for i in range(SIDE)]

    def at(dz, dx, dy):
        return zs[dz] * PLANE + xs[dx] * SIDE + ys[dy]

    barrier = pltpu.get_barrier_semaphore()

    def greet(target):
        pl.semaphore_signal(barrier, inc=1, device_id=(s, target), device_id_type=MESH)

    for load in loads[:4]:
        load.start()
    pl.semaphore_signal(barrier, inc=1, device_id=(1 - s, d), device_id_type=MESH)
    for dz, dx in PLANE_STEPS[:-1]:
        greet(zs[dz] * PLANE + xs[dx] * SIDE + z)
    for dx, turn in PLANE_STEPS:
        if turn:
            greet(y * PLANE + xs[dx] * SIDE + zs[turn])
    pl.when(y != z)(lambda: greet(z * PLANE + x * SIDE + z))
    for load in loads[4:]:
        load.start()

    query_load.wait()
    length_load.wait()
    key_load.wait()
    scores = lax.dot_general(
        query_ref[...], key_buf[...], (((1,), (1,)), ((), ())), preferred_element_type=jnp.float32
    ) * head_dim ** (-0.5)
    length = length_ref[0, d // SIDE]
    is_valid = lax.broadcasted_iota(jnp.int32, scores.shape, 1) < length
    scores = jnp.where(is_valid, scores, MASKED_SCORE)
    top = jnp.max(scores, axis=-1, keepdims=True)
    weights = jnp.where(is_valid, jnp.exp(scores - top), 0.0).astype(jnp.bfloat16)
    total = jnp.sum(weights.astype(jnp.float32), axis=-1, keepdims=True)
    value_load.wait()
    attended = jnp.dot(weights, value_buf[...], preferred_element_type=jnp.float32) / total
    att_out[...] = attended.reshape(att_out.shape)

    pl.semaphore_wait(barrier, 2 * PLANE - SIDE + 1 - (y == z).astype(jnp.int32))
    seq = d // SIDE
    for dx, dy in PLANE_STEPS:
        in_plane = xs[dx] * SIDE + ys[dy]
        src = att_out.at[in_plane]
        dst = att_in.at[seq]

        def send_row(src=src, dst=dst, target=y * PLANE + in_plane):
            pltpu.make_async_remote_copy(
                src, dst, att_send, att_recv, device_id=(s, target), device_id_type=MESH
            ).start()

        if (dx, dy) == (0, 0):
            pl.when(y != z)(send_row)

            @pl.when(y == z)
            def _():
                pltpu.make_async_copy(src, dst, att_recv).start()
        else:
            send_row()

    experts = router_buf.shape[0]
    route_load.wait()

    def match_of(routes):
        expert_row = lax.broadcasted_iota(jnp.int32, (experts, routes.shape[1]), 0)
        match = jnp.zeros(expert_row.shape, jnp.float32)
        for k in range(routes.shape[0]):
            match = match + (routes[k : k + 1] == expert_row).astype(jnp.float32)
        return match.astype(jnp.bfloat16)

    def exact_dot(left, right, left_dim=1, right_dim=0):
        return lax.dot_general(
            left.astype(jnp.bfloat16),
            right.astype(jnp.bfloat16),
            (((left_dim,), (right_dim,)), ((), ())),
            preferred_element_type=jnp.float32,
        )

    def iota(shape, dim):
        return lax.broadcasted_iota(jnp.int32, shape, dim)

    routes = jnp.concatenate([route_ref[0], route_ref[1]], axis=1)
    chosen_row = jnp.sum((routes == d).astype(jnp.float32), axis=0, keepdims=True)
    row_a, row_b = iota((rows, rows), 0), iota((rows, rows), 1)
    before = (row_a < row_b) & (row_a // seqs == row_b // seqs)
    rank_row = exact_dot(jnp.broadcast_to(chosen_row, (2 * CAP, rows)), before)
    slot, token = iota((2 * CAP, rows), 0), iota((2 * CAP, rows), 1)
    pick = (
        (token // seqs == slot // CAP)
        & (rank_row == lax.rem(slot, CAP).astype(jnp.float32))
        & (chosen_row > 0.5)
    )
    chosen = exact_dot(pick, match_of(routes), 1, 1)

    match_rows = match_of(route_ref[s])
    token_a, token_b = iota((seqs, seqs), 0), iota((seqs, seqs), 1)
    rank_rows = exact_dot(match_rows, token_a < token_b)
    wide = experts * CAP
    to_slots = iota((wide, experts), 0) // CAP == iota((wide, experts), 1)
    gather_rows = (exact_dot(to_slots, match_rows) > 0.5) & (
        exact_dot(to_slots, rank_rows) == lax.rem(iota((wide, seqs), 0), CAP).astype(jnp.float32)
    )
    match = exact_dot(token_a == token_b, match_rows, 1, 1)
    rank = exact_dot(token_a == token_b, rank_rows, 1, 1)
    slots = experts * 2
    spread = iota((experts, slots), 1) // 2 == iota((experts, slots), 0)
    match_slots = exact_dot(match, spread) > 0.5
    rank_slots = exact_dot(rank, spread)
    low_slot = lax.rem(iota((seqs, slots), 1), 2).astype(jnp.float32)
    scatter_rows = jnp.concatenate(
        [
            jnp.where(match_slots & (rank_slots == low_slot + 2.0 * i), 1.0, 0.0)
            for i in range(CAP // 2)
        ],
        axis=0,
    )

    out_weight_load.wait()
    pltpu.make_async_copy(att_in, att_in, att_recv).wait()
    head_rows = att_in[...].reshape(seqs, head_dim).astype(jnp.bfloat16)
    for dz in range(SIDE):
        base = pl.multiple_of(dz * chunk, chunk)
        partial = jnp.dot(
            head_rows, out_weight_buf[:, pl.ds(base, chunk)], preferred_element_type=jnp.float32
        ).astype(jnp.bfloat16)
        for j in range(chunk_blocks):
            part_out[dz * chunk_blocks + j] = partial[:, j * LANES : (j + 1) * LANES]
    odd = lax.rem(y, 2)
    shifts = (2 * odd, 2 * (1 - odd))
    block_z = [[lax.rem(z + i + shift, SIDE) for i in range(SIDE)] for shift in shifts]
    block_x = [[lax.rem(x + i + shift, SIDE) for i in range(SIDE)] for shift in shifts]

    def block_at(dz, dx, dy):
        place = block_z[dy % 2][dz] * SIDE + block_x[dy % 2][dx]
        return place * 2 + ys[dy] // 2

    for step in CUBE_STEPS:
        target = at(*step)
        src = part_out.at[block_at(*step)]
        dst = part_in.at[d]
        if step == (0, 0, 0):
            pltpu.make_async_copy(src, dst, part_recv).start()
        else:
            pltpu.make_async_remote_copy(
                src, dst, part_send, part_recv, device_id=(s, target), device_id_type=MESH
            ).start()

    my_block = block_at(0, 0, 0)
    lanes_at = pl.multiple_of(my_block * LANES, LANES)
    hidden_load.wait()
    gain_load.wait()
    hidden_block = hidden_ref[:, pl.ds(lanes_at, LANES)].astype(jnp.float32)
    gain = gain_ref[...].astype(jnp.float32)
    gain_buf[...] = gain
    inverse_buf[...] = 1.0 / (gain * gain)
    gain_block = gain_buf[pl.ds(my_block, 1), :]

    pltpu.make_async_copy(part_in, part_in, part_recv).wait()
    residual = hidden_block
    for i in range(part_in.shape[0]):
        residual = residual + part_in[i].astype(jnp.float32)
    block = (residual * gain_block).astype(jnp.bfloat16)
    block_rows = exact_dot(gather_rows, block)
    for e in range(experts):
        block_out[e] = block_rows[e * CAP : (e + 1) * CAP]

    turn = 1 - 2 * odd
    near_z = [lax.rem(z + turn * i + SIDE, SIDE) for i in range(SIDE)]
    near_x = [lax.rem(x + turn * i + SIDE, SIDE) for i in range(SIDE)]
    near_y = [lax.rem(y + turn * i + SIDE, SIDE) for i in range(SIDE)]
    for place, (dz, dx, dy) in enumerate(NEAR_STEPS):
        target = near_z[dz] * PLANE + near_x[dx] * SIDE + near_y[dy]
        src = block_out.at[target]
        dst = rows_in.at[place, s]
        arrival = rows_recv.at[place // BATCH]
        for group in (1 - s, s):
            if (dz, dx, dy) == (0, 0, 0) and group is s:
                pltpu.make_async_copy(src, dst, arrival).start()
            else:
                pltpu.make_async_remote_copy(
                    src, dst, rows_send, arrival, device_id=(group, target), device_id_type=MESH
                ).start()

    res_out[...] = residual
    res_copy = pltpu.make_async_remote_copy(
        res_out, res_in, res_send, res_recv, device_id=(s, d + turn), device_id_type=MESH
    )

    @pl.when(odd == 0)
    def _():
        res_in[...] = residual
        res_copy.start()

    gate_proj = jnp.zeros((2 * CAP, gate_buf.shape[1]), jnp.float32)
    up_proj = jnp.zeros((2 * CAP, gate_buf.shape[1]), jnp.float32)
    squares = jnp.zeros((2 * CAP, LANES), jnp.float32)
    logits = jnp.zeros((2 * CAP, experts), jnp.float32)
    router_load.wait()
    gate_load.wait()
    up_load.wait()
    def from_steps(center, shift, side):
        return [lax.rem(center + SIDE - (1 - 2 * side) * i + shift * side, SIDE) for i in range(SIDE)]

    sides = (odd, 1 - odd)
    from_z = [from_steps(z, 2, side) for side in sides]
    from_x = [from_steps(x, 2, side) for side in sides]
    from_y = [from_steps(y, 0, side) for side in sides]
    for place, (dz, dx, dy) in enumerate(NEAR_STEPS):
        if place % BATCH == 0:
            arrived = rows_in.at[pl.ds(place, BATCH)]
            pltpu.make_async_copy(arrived, arrived, rows_recv.at[place // BATCH]).wait()
        side = dy % 2
        row = (from_z[side][dz] * SIDE + from_x[side][dx]) * 2 + from_y[side][dy] // 2
        base = pl.multiple_of(row * LANES, LANES)
        picked_rows = rows_in[place].reshape(2 * CAP, LANES)
        tokens = picked_rows.astype(jnp.bfloat16)
        gate_proj = gate_proj + jnp.dot(
            tokens, gate_buf[pl.ds(base, LANES), :], preferred_element_type=jnp.float32
        )
        up_proj = up_proj + jnp.dot(
            tokens, up_buf[pl.ds(base, LANES), :], preferred_element_type=jnp.float32
        )
        logits = logits + lax.dot_general(
            tokens,
            router_buf[:, pl.ds(base, LANES)],
            (((1,), (1,)), ((), ())),
            preferred_element_type=jnp.float32,
        )
        squares = squares + picked_rows * picked_rows * inverse_buf[pl.ds(row, 1), :]
    scale = lax.rsqrt(jnp.sum(squares, axis=1, keepdims=True) / width + NORM_EPS)
    shares = chosen * jax.nn.sigmoid(logits * scale)
    share_sum = jnp.sum(shares, axis=1, keepdims=True)
    own_share = jnp.sum(
        jnp.where(iota(shares.shape, 1) == d, shares, 0.0), axis=1, keepdims=True
    )
    gates = jnp.where(share_sum > 0.0, own_share / share_sum, 0.0)
    gate_proj = gate_proj * scale
    up_proj = up_proj * scale
    packed = (gate_proj * jax.nn.sigmoid(gate_proj) * up_proj).astype(jnp.bfloat16)

    down_load.wait()
    low_lane = iota((CAP // 2, LANES), 1) < LANES // 2

    def down(plane, first_x, size):
        start = plane * chunk_blocks + first_x * 2
        product = gates * jnp.dot(
            packed,
            down_buf[:, start * LANES : (start + 2 * size) * LANES],
            preferred_element_type=jnp.float32,
        )
        for j in range(2 * size):
            block = product[:, j * LANES : (j + 1) * LANES]
            turned = pltpu.roll(block, LANES // 2, 1)
            owner = (start + j) * 2
            for batch in range(2):
                low = slice(batch * CAP, batch * CAP + CAP // 2)
                high = slice(batch * CAP + CAP // 2, (batch + 1) * CAP)
                comb_out[owner, batch] = jnp.where(low_lane, block[low], turned[high])
                comb_out[owner + 1, batch] = jnp.where(low_lane, turned[low], block[high])

    def combine(plane, first_x, size):
        for target_x in range(first_x, first_x + size):
            for dy in (2, 1, 3, 0):
                target = (plane * SIDE + target_x) * SIDE + ys[dy]
                dst = comb_in.at[s, d]
                for group in (1 - s, s):
                    src = comb_out.at[target, group]

                    def send_rows(src=src, dst=dst, group=group, target=target):
                        pltpu.make_async_remote_copy(
                            src, dst, comb_send, comb_recv, device_id=(group, target), device_id_type=MESH
                        ).start()

                    if dy == 0 and group is s:
                        pl.when(target != d)(send_rows)

                        @pl.when(target == d)
                        def _(src=src, dst=dst):
                            pltpu.make_async_copy(src, dst, comb_recv).start()
                    else:
                        send_rows()

    parts = [(0, 0, 1), (0, 1, 1), (0, 2, 2)] + [(plane, 0, 4) for plane in (1, 3, 2)]
    for part in parts:
        down(*part)
        combine(*part)

    pltpu.make_async_copy(comb_in, comb_in, comb_recv).wait()
    expert_rows = (comb_in[0] + comb_in[1]).reshape(slots, LANES)
    routed = jnp.dot(
        scatter_rows,
        expert_rows,
        precision=lax.Precision.HIGHEST,
        preferred_element_type=jnp.float32,
    )
    features = out_ref.shape[2]
    pl.when(odd == 1)(res_copy.wait_recv)
    residual = res_in[...]
    mixed = jnp.where(odd == 0, residual[:, :features], residual[:, features:])
    mixed = mixed + routed[:seqs, :features] + routed[seqs:, features:]
    out_ref[0] = mixed.astype(out_ref.dtype)

    most = att_in.at[pl.ds(0, PLANE - 1)]
    pltpu.make_async_copy(most, most, att_send).wait()

    @pl.when(y != z)
    def _():
        pltpu.make_async_copy(att_in.at[0], att_in.at[0], att_send).wait()

    most = part_in.at[pl.ds(0, SIDE * PLANE - 1)]
    pltpu.make_async_copy(most, most, part_send).wait()
    most = block_out.at[pl.ds(0, SIDE * PLANE - 1)]
    pltpu.make_async_copy(most, most, rows_send).wait()
    pl.when(odd == 0)(res_copy.wait_send)

    pltpu.make_async_copy(comb_in.at[0], comb_in.at[0], comb_send).wait()
    most = comb_in.at[0, pl.ds(0, SIDE * PLANE - 1)]
    pltpu.make_async_copy(most, most, comb_send).wait()


def body(
    hidden_in,
    queries,
    key_cache,
    value_cache,
    kv_lengths,
    route_ids,
    out_weight,
    norm_gain,
    router_weight,
    w_gate,
    w_up,
    w_down,
):
    seqs, width = hidden_in.shape[1:]
    kv_span, head_dim = key_cache.shape[2:]
    experts = router_weight.shape[1]
    hidden_units = w_gate.shape[2]
    devices = lax.axis_size("dev")
    blocks = width // LANES
    operands = (
        hidden_in,
        queries,
        key_cache,
        value_cache,
        kv_lengths,
        jnp.swapaxes(route_ids, 1, 2),
        out_weight,
        norm_gain.reshape(blocks, LANES),
        router_weight.T,
        w_gate,
        w_up,
        w_down,
    )
    dma = pltpu.SemaphoreType.DMA
    return pl.pallas_call(
        layer_kernel,
        out_shape=jax.ShapeDtypeStruct((1, seqs, width // devices), jnp.bfloat16),
        in_specs=[pl.BlockSpec(memory_space=pl.ANY)] * len(operands),
        out_specs=pl.BlockSpec(memory_space=pltpu.VMEM),
        scratch_shapes=[
            pltpu.VMEM((seqs, width), jnp.bfloat16),
            pltpu.VMEM(queries.shape[2:], jnp.bfloat16),
            pltpu.SMEM(kv_lengths.shape, jnp.int32),
            pltpu.VMEM((2, route_ids.shape[2], seqs), jnp.int32),
            pltpu.VMEM((blocks, LANES), jnp.bfloat16),
            pltpu.VMEM((kv_span, head_dim), jnp.bfloat16),
            pltpu.VMEM((kv_span, head_dim), jnp.bfloat16),
            pltpu.VMEM(out_weight.shape, jnp.bfloat16),
            pltpu.VMEM((experts, width), jnp.bfloat16),
            pltpu.VMEM((width, hidden_units), jnp.bfloat16),
            pltpu.VMEM((width, hidden_units), jnp.bfloat16),
            pltpu.VMEM((hidden_units, width), jnp.bfloat16),
            pltpu.VMEM((seqs, 1, head_dim), jnp.float32),
            pltpu.VMEM((seqs, 1, head_dim), jnp.float32),
            pltpu.VMEM((blocks, seqs, LANES), jnp.bfloat16),
            pltpu.VMEM((devices, seqs, LANES), jnp.bfloat16),
            pltpu.VMEM((experts, CAP, LANES), jnp.float32),
            pltpu.VMEM((blocks, 2, CAP, LANES), jnp.float32),
            pltpu.VMEM((blocks, LANES), jnp.float32),
            pltpu.VMEM((blocks, LANES), jnp.float32),
            pltpu.VMEM((seqs, LANES), jnp.float32),
            pltpu.VMEM((seqs, LANES), jnp.float32),
            pltpu.VMEM((devices, 2, CAP // 2, LANES), jnp.float32),
            pltpu.VMEM((2, devices, CAP // 2, LANES), jnp.float32),
            dma((12,)),
            dma,
            dma,
            dma,
            dma,
            dma,
            dma((blocks // BATCH,)),
            dma,
            dma,
            dma,
            dma,
        ],
        compiler_params=pltpu.CompilerParams(
            collective_id=0, has_side_effects=True, vmem_limit_bytes=32 * 2**20
        ),
    )(*[pltpu.with_memory_space_constraint(operand, pltpu.HBM) for operand in operands])


def solution(mesh):
    placed = (
        P("sec", None, None),
        P("sec", "dev", None, None),
        P("sec", "dev", None, None),
        P("sec", "dev", None, None),
        P("sec", None),
        P(),
        P("dev", None),
        P(),
        P(),
        P("dev", None, "sec"),
        P("dev", None, "sec"),
        P("dev", "sec", None),
    )
    return jax.shard_map(
        body, mesh=mesh, in_specs=placed, out_specs=P("sec", None, "dev"), check_vma=False
    )
```

```python
import jax
import jax.numpy as jnp
from jax import lax
from jax.experimental import pallas as pl
from jax.experimental.pallas import tpu as pltpu
from jax.sharding import PartitionSpec as P

MASKED_SCORE = -1e30
NORM_EPS = 1e-06
MESH = pl.DeviceIdType.MESH
LANES = 128
CAP = 4
SIDE = 4
PLANE = SIDE * SIDE
BATCH = 2


def hops(step):
    return min(step, SIDE - step)


def far_first(steps):
    return sorted(steps, key=lambda step: -sum(hops(part) for part in step))


PLANE_STEPS = far_first([(dx, dy) for dx in range(SIDE) for dy in range(SIDE)])
CUBE_STEPS = far_first(
    [(dz, dx, dy) for dz in range(SIDE) for dx in range(SIDE) for dy in range(SIDE)]
)

SUM_STEPS = sorted(
    CUBE_STEPS, key=lambda p: (-sum(map(hops, p)), (p[0] * 7 + p[1] * 3 + p[2] * 5) % 11)
)

NEAR_STEPS = [
    (dz, dx, dy)
    for dz, dx, dy in CUBE_STEPS[::-1]
    if hops(dz) + hops(dx) + hops(dy) < hops((dz + 2) % 4) + hops((dx + 2) % 4) + hops((dy + 3) % 4)
]


def layer_kernel(
    hidden_hbm,
    query_hbm,
    key_hbm,
    value_hbm,
    length_hbm,
    route_hbm,
    out_weight_hbm,
    gain_hbm,
    router_hbm,
    gate_hbm,
    up_hbm,
    down_hbm,
    out_ref,
    hidden_ref,
    query_ref,
    length_ref,
    route_ref,
    gain_ref,
    key_buf,
    value_buf,
    out_weight_buf,
    router_buf,
    gate_buf,
    up_buf,
    down_buf,
    att_out,
    att_in,
    part_out,
    part_in,
    block_out,
    rows_in,
    gain_buf,
    inverse_buf,
    res_out,
    res_in,
    comb_out,
    comb_in,
    load_sem,
    att_send,
    att_recv,
    part_send,
    part_recv,
    rows_send,
    rows_recv,
    res_send,
    res_recv,
    comb_send,
    comb_recv,
):
    s = lax.axis_index("sec")
    d = lax.axis_index("dev")
    z = d // PLANE
    x = lax.rem(d // SIDE, SIDE)
    y = lax.rem(d, SIDE)
    seqs = hidden_ref.shape[0]
    head_dim = key_buf.shape[1]
    width = out_weight_buf.shape[1]
    rows = 2 * seqs
    chunk = width // SIDE
    chunk_blocks = chunk // LANES

    loads = [
        pltpu.make_async_copy(src, dst, load_sem.at[i])
        for i, (src, dst) in enumerate(
            (
                (length_hbm, length_ref),
                (query_hbm.at[0, 0], query_ref),
                (key_hbm.at[0, 0], key_buf),
                (value_hbm.at[0, 0], value_buf),
                (route_hbm, route_ref),
                (out_weight_hbm, out_weight_buf),
                (gate_hbm.at[0], gate_buf),
                (up_hbm.at[0], up_buf),
                (router_hbm, router_buf),
                (down_hbm.at[0], down_buf),
                (hidden_hbm.at[0], hidden_ref),
                (gain_hbm, gain_ref),
            )
        )
    ]
    (
        length_load,
        query_load,
        key_load,
        value_load,
        route_load,
        out_weight_load,
        gate_load,
        up_load,
        router_load,
        down_load,
        hidden_load,
        gain_load,
    ) = loads
    zs = [lax.rem(z + i, SIDE) for i in range(SIDE)]
    xs = [lax.rem(x + i, SIDE) for i in range(SIDE)]
    ys = [lax.rem(y + i, SIDE) for i in range(SIDE)]

    def at(dz, dx, dy):
        return zs[dz] * PLANE + xs[dx] * SIDE + ys[dy]

    barrier = pltpu.get_barrier_semaphore()

    def greet(target):
        pl.semaphore_signal(barrier, inc=1, device_id=(s, target), device_id_type=MESH)

    for load in loads[:4]:
        load.start()
    pl.semaphore_signal(barrier, inc=1, device_id=(1 - s, d), device_id_type=MESH)
    for dz, dx in PLANE_STEPS[:-1]:
        greet(zs[dz] * PLANE + xs[dx] * SIDE + z)
    for dx, turn in PLANE_STEPS:
        if turn:
            greet(y * PLANE + xs[dx] * SIDE + zs[turn])
    pl.when(y != z)(lambda: greet(z * PLANE + x * SIDE + z))
    for load in loads[4:]:
        load.start()

    query_load.wait()
    length_load.wait()
    key_load.wait()
    scores = lax.dot_general(
        query_ref[...], key_buf[...], (((1,), (1,)), ((), ())), preferred_element_type=jnp.float32
    ) * head_dim ** (-0.5)
    length = length_ref[0, d // SIDE]
    is_valid = lax.broadcasted_iota(jnp.int32, scores.shape, 1) < length
    scores = jnp.where(is_valid, scores, MASKED_SCORE)
    top = jnp.max(scores, axis=-1, keepdims=True)
    weights = jnp.where(is_valid, jnp.exp(scores - top), 0.0).astype(jnp.bfloat16)
    total = jnp.sum(weights.astype(jnp.float32), axis=-1, keepdims=True)
    value_load.wait()
    attended = jnp.dot(weights, value_buf[...], preferred_element_type=jnp.float32) / total
    att_out[...] = attended.reshape(att_out.shape)

    pl.semaphore_wait(barrier, 2 * PLANE - SIDE + 1 - (y == z).astype(jnp.int32))
    seq = d // SIDE
    for dx, dy in PLANE_STEPS:
        in_plane = xs[dx] * SIDE + ys[dy]
        src = att_out.at[in_plane]
        dst = att_in.at[seq]

        def send_row(src=src, dst=dst, target=y * PLANE + in_plane):
            pltpu.make_async_remote_copy(
                src, dst, att_send, att_recv, device_id=(s, target), device_id_type=MESH
            ).start()

        if (dx, dy) == (0, 0):
            pl.when(y != z)(send_row)

            @pl.when(y == z)
            def _():
                pltpu.make_async_copy(src, dst, att_recv).start()
        else:
            send_row()

    experts = router_buf.shape[0]
    route_load.wait()

    def match_of(routes):
        expert_row = lax.broadcasted_iota(jnp.int32, (experts, routes.shape[1]), 0)
        match = jnp.zeros(expert_row.shape, jnp.float32)
        for k in range(routes.shape[0]):
            match = match + (routes[k : k + 1] == expert_row).astype(jnp.float32)
        return match.astype(jnp.bfloat16)

    def exact_dot(left, right, left_dim=1, right_dim=0):
        return lax.dot_general(
            left.astype(jnp.bfloat16),
            right.astype(jnp.bfloat16),
            (((left_dim,), (right_dim,)), ((), ())),
            preferred_element_type=jnp.float32,
        )

    def iota(shape, dim):
        return lax.broadcasted_iota(jnp.int32, shape, dim)

    routes = jnp.concatenate([route_ref[0], route_ref[1]], axis=1)
    chosen_row = jnp.sum((routes == d).astype(jnp.float32), axis=0, keepdims=True)
    row_a, row_b = iota((rows, rows), 0), iota((rows, rows), 1)
    before = (row_a < row_b) & (row_a // seqs == row_b // seqs)
    rank_row = exact_dot(jnp.broadcast_to(chosen_row, (2 * CAP, rows)), before)
    slot, token = iota((2 * CAP, rows), 0), iota((2 * CAP, rows), 1)
    pick = (
        (token // seqs == slot // CAP)
        & (rank_row == lax.rem(slot, CAP).astype(jnp.float32))
        & (chosen_row > 0.5)
    )
    chosen = exact_dot(pick, match_of(routes), 1, 1)

    match_rows = match_of(route_ref[s])
    token_a, token_b = iota((seqs, seqs), 0), iota((seqs, seqs), 1)
    rank_rows = exact_dot(match_rows, token_a < token_b)
    wide = experts * CAP
    to_slots = iota((wide, experts), 0) // CAP == iota((wide, experts), 1)
    gather_rows = (exact_dot(to_slots, match_rows) > 0.5) & (
        exact_dot(to_slots, rank_rows) == lax.rem(iota((wide, seqs), 0), CAP).astype(jnp.float32)
    )
    match = exact_dot(token_a == token_b, match_rows, 1, 1)
    rank = exact_dot(token_a == token_b, rank_rows, 1, 1)
    slots = experts * 2
    spread = iota((experts, slots), 1) // 2 == iota((experts, slots), 0)
    match_slots = exact_dot(match, spread) > 0.5
    rank_slots = exact_dot(rank, spread)
    low_slot = lax.rem(iota((seqs, slots), 1), 2).astype(jnp.float32)
    scatter_rows = jnp.concatenate(
        [
            jnp.where(match_slots & (rank_slots == low_slot + 2.0 * i), 1.0, 0.0)
            for i in range(CAP // 2)
        ],
        axis=0,
    )

    out_weight_load.wait()
    pltpu.make_async_copy(att_in, att_in, att_recv).wait()
    head_rows = att_in[...].reshape(seqs, head_dim).astype(jnp.bfloat16)
    for dz in range(SIDE):
        base = pl.multiple_of(dz * chunk, chunk)
        partial = jnp.dot(
            head_rows, out_weight_buf[:, pl.ds(base, chunk)], preferred_element_type=jnp.float32
        ).astype(jnp.bfloat16)
        for j in range(chunk_blocks):
            part_out[dz * chunk_blocks + j] = partial[:, j * LANES : (j + 1) * LANES]
    odd = lax.rem(y, 2)
    shifts = (2 * odd, 2 * (1 - odd))
    block_z = [[lax.rem(z + i + shift, SIDE) for i in range(SIDE)] for shift in shifts]
    block_x = [[lax.rem(x + i + shift, SIDE) for i in range(SIDE)] for shift in shifts]

    def block_at(dz, dx, dy):
        place = block_z[dy % 2][dz] * SIDE + block_x[dy % 2][dx]
        return place * 2 + ys[dy] // 2

    for step in SUM_STEPS:
        target = at(*step)
        src = part_out.at[block_at(*step)]
        dst = part_in.at[d]
        if step == (0, 0, 0):
            pltpu.make_async_copy(src, dst, part_recv).start()
        else:
            pltpu.make_async_remote_copy(
                src, dst, part_send, part_recv, device_id=(s, target), device_id_type=MESH
            ).start()

    my_block = block_at(0, 0, 0)
    lanes_at = pl.multiple_of(my_block * LANES, LANES)
    hidden_load.wait()
    gain_load.wait()
    hidden_block = hidden_ref[:, pl.ds(lanes_at, LANES)].astype(jnp.float32)
    gain = gain_ref[...].astype(jnp.float32)
    gain_buf[...] = gain
    inverse_buf[...] = 1.0 / (gain * gain)
    gain_block = gain_buf[pl.ds(my_block, 1), :]

    pltpu.make_async_copy(part_in, part_in, part_recv).wait()
    residual = hidden_block
    for i in range(part_in.shape[0]):
        residual = residual + part_in[i].astype(jnp.float32)
    block = (residual * gain_block).astype(jnp.bfloat16)
    block_rows = exact_dot(gather_rows, block)
    for e in range(experts):
        block_out[e] = block_rows[e * CAP : (e + 1) * CAP]

    turn = 1 - 2 * odd
    near_z = [lax.rem(z + turn * i + SIDE, SIDE) for i in range(SIDE)]
    near_x = [lax.rem(x + turn * i + SIDE, SIDE) for i in range(SIDE)]
    near_y = [lax.rem(y + turn * i + SIDE, SIDE) for i in range(SIDE)]
    for place, (dz, dx, dy) in enumerate(NEAR_STEPS):
        target = near_z[dz] * PLANE + near_x[dx] * SIDE + near_y[dy]
        src = block_out.at[target]
        dst = rows_in.at[place, s]
        arrival = rows_recv.at[place // BATCH]
        for group in (1 - s, s):
            if (dz, dx, dy) == (0, 0, 0) and group is s:
                pltpu.make_async_copy(src, dst, arrival).start()
            else:
                pltpu.make_async_remote_copy(
                    src, dst, rows_send, arrival, device_id=(group, target), device_id_type=MESH
                ).start()

    res_out[...] = residual
    res_copy = pltpu.make_async_remote_copy(
        res_out, res_in, res_send, res_recv, device_id=(s, d + turn), device_id_type=MESH
    )

    @pl.when(odd == 0)
    def _():
        res_in[...] = residual
        res_copy.start()

    gate_proj = jnp.zeros((2 * CAP, gate_buf.shape[1]), jnp.float32)
    up_proj = jnp.zeros((2 * CAP, gate_buf.shape[1]), jnp.float32)
    squares = jnp.zeros((2 * CAP, LANES), jnp.float32)
    logits = jnp.zeros((2 * CAP, experts), jnp.float32)
    router_load.wait()
    gate_load.wait()
    up_load.wait()
    def from_steps(center, shift, side):
        return [lax.rem(center + SIDE - (1 - 2 * side) * i + shift * side, SIDE) for i in range(SIDE)]

    sides = (odd, 1 - odd)
    from_z = [from_steps(z, 2, side) for side in sides]
    from_x = [from_steps(x, 2, side) for side in sides]
    from_y = [from_steps(y, 0, side) for side in sides]
    for place, (dz, dx, dy) in enumerate(NEAR_STEPS):
        if place % BATCH == 0:
            arrived = rows_in.at[pl.ds(place, BATCH)]
            pltpu.make_async_copy(arrived, arrived, rows_recv.at[place // BATCH]).wait()
        side = dy % 2
        row = (from_z[side][dz] * SIDE + from_x[side][dx]) * 2 + from_y[side][dy] // 2
        base = pl.multiple_of(row * LANES, LANES)
        picked_rows = rows_in[place].reshape(2 * CAP, LANES)
        tokens = picked_rows.astype(jnp.bfloat16)
        gate_proj = gate_proj + jnp.dot(
            tokens, gate_buf[pl.ds(base, LANES), :], preferred_element_type=jnp.float32
        )
        up_proj = up_proj + jnp.dot(
            tokens, up_buf[pl.ds(base, LANES), :], preferred_element_type=jnp.float32
        )
        logits = logits + lax.dot_general(
            tokens,
            router_buf[:, pl.ds(base, LANES)],
            (((1,), (1,)), ((), ())),
            preferred_element_type=jnp.float32,
        )
        squares = squares + picked_rows * picked_rows * inverse_buf[pl.ds(row, 1), :]
    scale = lax.rsqrt(jnp.sum(squares, axis=1, keepdims=True) / width + NORM_EPS)
    shares = chosen * jax.nn.sigmoid(logits * scale)
    share_sum = jnp.sum(shares, axis=1, keepdims=True)
    own_share = jnp.sum(
        jnp.where(iota(shares.shape, 1) == d, shares, 0.0), axis=1, keepdims=True
    )
    gates = jnp.where(share_sum > 0.0, own_share / share_sum, 0.0)
    gate_proj = gate_proj * scale
    up_proj = up_proj * scale
    packed = (gate_proj * jax.nn.sigmoid(gate_proj) * up_proj).astype(jnp.bfloat16)

    down_load.wait()
    low_lane = iota((CAP // 2, LANES), 1) < LANES // 2

    def down(plane, first_x, size):
        start = plane * chunk_blocks + first_x * 2
        product = gates * jnp.dot(
            packed,
            down_buf[:, start * LANES : (start + 2 * size) * LANES],
            preferred_element_type=jnp.float32,
        )
        for j in range(2 * size):
            block = product[:, j * LANES : (j + 1) * LANES]
            turned = pltpu.roll(block, LANES // 2, 1)
            owner = (start + j) * 2
            for batch in range(2):
                low = slice(batch * CAP, batch * CAP + CAP // 2)
                high = slice(batch * CAP + CAP // 2, (batch + 1) * CAP)
                comb_out[owner, batch] = jnp.where(low_lane, block[low], turned[high])
                comb_out[owner + 1, batch] = jnp.where(low_lane, turned[low], block[high])

    def combine(plane, first_x, size):
        for target_x in range(first_x, first_x + size):
            nearest = plane == 0
            for dy in (0, 1, 3, 2) if nearest else (2, 1, 3, 0):
                target = (plane * SIDE + target_x) * SIDE + (dy if nearest else ys[dy])
                dst = comb_in.at[s, d]
                for group in (1 - s, s):
                    src = comb_out.at[target, group]

                    def send_rows(src=src, dst=dst, group=group, target=target):
                        pltpu.make_async_remote_copy(
                            src, dst, comb_send, comb_recv, device_id=(group, target), device_id_type=MESH
                        ).start()

                    if (nearest or dy == 0) and group is s:
                        pl.when(target != d)(send_rows)

                        @pl.when(target == d)
                        def _(src=src, dst=dst):
                            pltpu.make_async_copy(src, dst, comb_recv).start()
                    else:
                        send_rows()

    parts = [(0, 0, 1), (0, 1, 1), (0, 2, 2)] + [(plane, 0, 4) for plane in (1, 3, 2)]
    for part in parts:
        down(*part)
        combine(*part)

    pltpu.make_async_copy(comb_in, comb_in, comb_recv).wait()
    expert_rows = (comb_in[0] + comb_in[1]).reshape(slots, LANES)
    high_rows = expert_rows.astype(jnp.bfloat16)
    low_rows = expert_rows - high_rows.astype(jnp.float32)
    routed = exact_dot(scatter_rows, high_rows) + exact_dot(scatter_rows, low_rows)
    features = out_ref.shape[2]
    pl.when(odd == 1)(res_copy.wait_recv)
    residual = res_in[...]
    mixed = jnp.where(odd == 0, residual[:, :features], residual[:, features:])
    mixed = mixed + routed[:seqs, :features] + routed[seqs:, features:]
    out_ref[0] = mixed.astype(out_ref.dtype)

    most = att_in.at[pl.ds(0, PLANE - 1)]
    pltpu.make_async_copy(most, most, att_send).wait()

    @pl.when(y != z)
    def _():
        pltpu.make_async_copy(att_in.at[0], att_in.at[0], att_send).wait()

    most = part_in.at[pl.ds(0, SIDE * PLANE - 1)]
    pltpu.make_async_copy(most, most, part_send).wait()
    most = block_out.at[pl.ds(0, SIDE * PLANE - 1)]
    pltpu.make_async_copy(most, most, rows_send).wait()
    pl.when(odd == 0)(res_copy.wait_send)

    pltpu.make_async_copy(comb_in.at[0], comb_in.at[0], comb_send).wait()
    most = comb_in.at[0, pl.ds(0, SIDE * PLANE - 1)]
    pltpu.make_async_copy(most, most, comb_send).wait()


def body(
    hidden_in,
    queries,
    key_cache,
    value_cache,
    kv_lengths,
    route_ids,
    out_weight,
    norm_gain,
    router_weight,
    w_gate,
    w_up,
    w_down,
):
    seqs, width = hidden_in.shape[1:]
    kv_span, head_dim = key_cache.shape[2:]
    experts = router_weight.shape[1]
    hidden_units = w_gate.shape[2]
    devices = lax.axis_size("dev")
    blocks = width // LANES
    operands = (
        hidden_in,
        queries,
        key_cache,
        value_cache,
        kv_lengths,
        jnp.swapaxes(route_ids, 1, 2),
        out_weight,
        norm_gain.reshape(blocks, LANES),
        router_weight.T,
        w_gate,
        w_up,
        w_down,
    )
    dma = pltpu.SemaphoreType.DMA
    return pl.pallas_call(
        layer_kernel,
        out_shape=jax.ShapeDtypeStruct((1, seqs, width // devices), jnp.bfloat16),
        in_specs=[pl.BlockSpec(memory_space=pl.ANY)] * len(operands),
        out_specs=pl.BlockSpec(memory_space=pltpu.VMEM),
        scratch_shapes=[
            pltpu.VMEM((seqs, width), jnp.bfloat16),
            pltpu.VMEM(queries.shape[2:], jnp.bfloat16),
            pltpu.SMEM(kv_lengths.shape, jnp.int32),
            pltpu.VMEM((2, route_ids.shape[2], seqs), jnp.int32),
            pltpu.VMEM((blocks, LANES), jnp.bfloat16),
            pltpu.VMEM((kv_span, head_dim), jnp.bfloat16),
            pltpu.VMEM((kv_span, head_dim), jnp.bfloat16),
            pltpu.VMEM(out_weight.shape, jnp.bfloat16),
            pltpu.VMEM((experts, width), jnp.bfloat16),
            pltpu.VMEM((width, hidden_units), jnp.bfloat16),
            pltpu.VMEM((width, hidden_units), jnp.bfloat16),
            pltpu.VMEM((hidden_units, width), jnp.bfloat16),
            pltpu.VMEM((seqs, 1, head_dim), jnp.float32),
            pltpu.VMEM((seqs, 1, head_dim), jnp.float32),
            pltpu.VMEM((blocks, seqs, LANES), jnp.bfloat16),
            pltpu.VMEM((devices, seqs, LANES), jnp.bfloat16),
            pltpu.VMEM((experts, CAP, LANES), jnp.float32),
            pltpu.VMEM((blocks, 2, CAP, LANES), jnp.float32),
            pltpu.VMEM((blocks, LANES), jnp.float32),
            pltpu.VMEM((blocks, LANES), jnp.float32),
            pltpu.VMEM((seqs, LANES), jnp.float32),
            pltpu.VMEM((seqs, LANES), jnp.float32),
            pltpu.VMEM((devices, 2, CAP // 2, LANES), jnp.float32),
            pltpu.VMEM((2, devices, CAP // 2, LANES), jnp.float32),
            dma((12,)),
            dma,
            dma,
            dma,
            dma,
            dma,
            dma((blocks // BATCH,)),
            dma,
            dma,
            dma,
            dma,
        ],
        compiler_params=pltpu.CompilerParams(
            collective_id=0, has_side_effects=True, vmem_limit_bytes=32 * 2**20
        ),
    )(*[pltpu.with_memory_space_constraint(operand, pltpu.HBM) for operand in operands])


def solution(mesh):
    placed = (
        P("sec", None, None),
        P("sec", "dev", None, None),
        P("sec", "dev", None, None),
        P("sec", "dev", None, None),
        P("sec", None),
        P(),
        P("dev", None),
        P(),
        P(),
        P("dev", None, "sec"),
        P("dev", None, "sec"),
        P("dev", "sec", None),
    )
    return jax.shard_map(
        body, mesh=mesh, in_specs=placed, out_specs=P("sec", None, "dev"), check_vma=False
    )
```
